128 devices in a mesh: row: 16 (over y_lo, z, core), col: 8 (over y_hi, x).
Axes of the slice: x: 4, y: 4 (y_hi: 2, y_lo: 2; y = y_hi * 2 + y_lo), z: 4, core: 2. Of those that a mesh axis runs over, the one named last changes fastest.
Arguments:
- features: bfloat16 [98304, 256], P(('col', 'row')), may hold values from -6 to 6
- weight: bfloat16 [256, 256], replicated, may hold values from -0.375 to 0.375
- grad_out: bfloat16 [98304, 256], P(('row', 'col')), may hold values from -6 to 6
- tile_rows: int32 [16, 8, 608], P('row', 'col'), may hold values from 0 to 95
- tile_cols: int32 [16, 8, 608], P('row', 'col'), may hold values from 0 to 191
- tile_values: bfloat16 [16, 8, 608, 4096], P('row', 'col'), may hold values from 0 to 0.1, as said below
- tile_counts: int32 [16, 8], P('row', 'col'), may hold values from 76 to 608, as said below
Outputs:
- output: bfloat16 [98304, 256], P(('row', 'col'))
- grad_feat: bfloat16 [98304, 256], P(('col', 'row'))
- grad_weight: float32 [256, 256], replicated
The draws below stay inside these ranges and needn't reach their ends.
Inputs may be any that keep to these rules, and one draw needn't show every extreme that they name: `tile_values`: tile values are zero or positive; about 3 percent of a tile's entries are nonzero, lying in about a quarter of its rows and a quarter of its columns. `tile_counts`: each count is 608, 304, 152 or 76, and some device holds 608.
All inputs are finite; a program needn't handle non-finite values.
Results may differ from the reference program's by a relative error of at most 0.022.
Values may be sent and summed in bfloat16 or wider, within the bound.
A program may use at most 192 MiB of HBM per device.

```python
import jax
import jax.numpy as jnp
from jax import lax

D = 256
BLOCK = 64
GROUP = 152
TILES_DEV = 608
NODES = 98304
BLOCK_ROWS = 96
BLOCK_COLS = 192
N_ROW = 16
N_COL = 8


def draw_tile_values(key, part):
    key = jax.random.fold_in(key, 11)
    first, second, third, fourth = jax.random.split(key, 4)
    lead = (N_ROW, N_COL, TILES_DEV)
    row_live = jax.random.bernoulli(first, 0.25, lead + (BLOCK, 1))
    col_live = jax.random.bernoulli(second, 0.25, lead + (1, BLOCK))
    keep = jax.random.bernoulli(third, 0.5, lead + (BLOCK, BLOCK))
    keep = jnp.logical_and(keep, jnp.logical_and(row_live, col_live))
    shape = lead + (BLOCK, BLOCK)
    magnitude = jax.random.uniform(fourth, shape, jnp.float32, 0.02, 0.06)
    values = jnp.where(keep, magnitude, 0.0)
    return values.reshape(lead + (BLOCK * BLOCK,)).astype(jnp.bfloat16)


def draw_tile_counts(key, part):
    key = jax.random.fold_in(key, 12)
    first, second = jax.random.split(key)
    shifts = jax.random.randint(first, (N_ROW * N_COL,), 0, 4)
    counts = jnp.right_shift(jnp.full((N_ROW * N_COL,), TILES_DEV, jnp.int32), shifts.astype(jnp.int32))
    chosen = jax.random.randint(second, (), 0, N_ROW * N_COL)
    counts = counts.at[chosen].set(TILES_DEV)
    return counts.reshape(N_ROW, N_COL).astype(jnp.int32)


def touch_ends(result, stream_key, smallest, high):
    longest = result.shape.index(max(result.shape))
    spots = []
    for shift in (0, 1):
        where = [jax.random.randint(jax.random.fold_in(stream_key, axis), (), 0, length) for axis, length in enumerate(result.shape)]
        where[longest] = (where[longest] + shift) % result.shape[longest]
        spots.append(tuple(where))
    return result.at[spots[0]].set(smallest).at[spots[1]].set(high)


def steps_of(own_key, dims, cuts, smallest, high):
    loudness = 1.0
    for dim, parts in cuts:
        heights = jax.random.uniform(jax.random.fold_in(jax.random.fold_in(own_key, 6), dim), (parts,), jnp.float32, smallest / len(cuts), high / len(cuts))
        loudness = loudness * jnp.repeat(jnp.exp(heights), dims[dim] // parts).reshape((-1,) + (1,) * (len(dims) - 1 - dim))
    return loudness


def normal_values(rng, extent, spread, bound, shards=(), held_as=jnp.bfloat16):
    level = steps_of(rng, extent, shards, -0.22, 0.18) if shards else 1.0
    result = jax.random.normal(rng, extent, jnp.float32) * spread * level
    return jnp.minimum(jnp.maximum(result, -bound), bound).astype(held_as)


def setup_inputs(seed: int = 0) -> dict:
    splits = jax.random.split(jax.random.key(seed), 8)
    return {
        "features": normal_values(splits[0], (NODES, D), 1.0, 6.0, ((0, 128),)),
        "weight": normal_values(splits[1], (D, D), D ** -0.5, 0.375),
        "grad_out": normal_values(splits[2], (NODES, D), 1.0, 6.0, ((0, 128),)),
        "tile_rows": touch_ends(jax.random.randint(splits[3], (N_ROW, N_COL, TILES_DEV), 0, BLOCK_ROWS), jax.random.fold_in(splits[3], 1), 0, BLOCK_ROWS - 1).astype(jnp.int32),
        "tile_cols": touch_ends(jax.random.randint(splits[4], (N_ROW, N_COL, TILES_DEV), 0, BLOCK_COLS), jax.random.fold_in(splits[4], 1), 0, BLOCK_COLS - 1).astype(jnp.int32),
        "tile_values": draw_tile_values(jax.random.fold_in(splits[7], 71), 0),
        "tile_counts": draw_tile_counts(jax.random.fold_in(splits[7], 71), 0),
    }


def activate(z):
    return jax.nn.gelu(z, approximate=True)

def round_trip(x):
    y = x.astype(jnp.bfloat16)
    y = lax.optimization_barrier(y)
    return y.astype(jnp.float32)

def tile_sum(values, rows, cols, count, source, out_blocks, flip):
    tiles = values.shape[0]
    group = min(GROUP, tiles)
    blocks = values.reshape(tiles, BLOCK, BLOCK)
    width = source.shape[1]
    pieces = source.reshape(-1, BLOCK, width)
    take, put = (rows, cols) if flip else (cols, rows)

    def step(index, total):
        start = (index * group).astype(jnp.int32)
        chosen = lax.dynamic_slice_in_dim(blocks, start, group, 0)
        take_now = lax.dynamic_slice_in_dim(take, start, group, 0)
        put_now = lax.dynamic_slice_in_dim(put, start, group, 0)
        live = start + jnp.arange(group, dtype=jnp.int32) < count
        chosen = jnp.where(live[:, None, None], chosen, jnp.zeros_like(chosen)).astype(jnp.float32)
        picked = pieces[take_now].astype(jnp.float32)
        if flip:
            product = jnp.einsum('tji,tjd->tid', chosen, picked)
        else:
            product = jnp.einsum('tij,tjd->tid', chosen, picked)
        return total.at[put_now].add(product)
    steps_needed = ((count + group - 1) // group).astype(jnp.int32)
    total = lax.fori_loop(jnp.int32(0), steps_needed, step, jnp.zeros((out_blocks, BLOCK, width), jnp.float32))
    return total.reshape(out_blocks * BLOCK, width)

def reference(features, weight, grad_out, tile_rows, tile_cols, tile_values, tile_counts):
    rows_group = NODES // N_ROW
    cols_group = NODES // N_COL

    def row_block(r):
        total = jnp.zeros((rows_group, D), jnp.float32)
        for c in range(N_COL):
            source = features[c * cols_group:(c + 1) * cols_group]
            part = tile_sum(tile_values[r, c], tile_rows[r, c], tile_cols[r, c], tile_counts[r, c], source, rows_group // BLOCK, False)
            total = total + round_trip(part)
        return total.astype(jnp.bfloat16)
    hidden = lax.map(row_block, jnp.arange(N_ROW, dtype=jnp.int32)).reshape(NODES, D)
    pre = jnp.dot(hidden, weight, preferred_element_type=jnp.float32)
    output = activate(pre).astype(jnp.bfloat16)
    grad_pre = jax.vjp(activate, pre)[1](grad_out.astype(jnp.float32))[0].astype(jnp.bfloat16)
    grad_weight = jnp.dot(hidden.T, grad_pre, preferred_element_type=jnp.float32)
    grad_hidden = jnp.dot(grad_pre, weight.T, preferred_element_type=jnp.float32).astype(jnp.bfloat16)

    def col_block(c):

        def add(r, total):
            source = lax.dynamic_slice_in_dim(grad_hidden, (r * rows_group).astype(jnp.int32), rows_group, 0)
            part = tile_sum(tile_values[r, c], tile_rows[r, c], tile_cols[r, c], tile_counts[r, c], source, cols_group // BLOCK, True)
            return total + round_trip(part)
        total = lax.fori_loop(jnp.int32(0), jnp.int32(N_ROW), add, jnp.zeros((cols_group, D), jnp.float32))
        return total.astype(jnp.bfloat16)
    grad_feat = lax.map(col_block, jnp.arange(N_COL, dtype=jnp.int32)).reshape(NODES, D)
    return (output, grad_feat, grad_weight)
```

```python
import functools
import jax, jax.numpy as jnp
from jax import lax
from jax.experimental import pallas as pl
from jax.experimental.pallas import tpu as pltpu
from jax.sharding import PartitionSpec as P

BLOCK = 64
GROUP = 4
f32, bf16, i32 = jnp.float32, jnp.bfloat16, jnp.int32


def meta_one(key_row, other_row, tiles, nb, slots):
    tp = key_row.shape[1]
    nbp = -(-nb // 128) * 128
    hot = lax.broadcasted_iota(i32, (nbp, tp), 0) == key_row
    hotf = hot.astype(f32)
    hotb = hotf.astype(bf16)
    count = jnp.sum(hotf, axis=1, keepdims=True)
    upper = (lax.broadcasted_iota(i32, (tp, tp), 0) < lax.broadcasted_iota(i32, (tp, tp), 1)).astype(f32).astype(bf16)
    rank = jnp.dot(hotb, upper, preferred_element_type=f32)
    groups = jnp.floor((count + (GROUP - 1)) * (1.0 / GROUP))
    lower = (lax.broadcasted_iota(i32, (nbp, nbp), 1) < lax.broadcasted_iota(i32, (nbp, nbp), 0)).astype(f32).astype(bf16)
    first = jnp.dot(lower, jnp.broadcast_to(groups, (nbp, 128)).astype(bf16), preferred_element_type=f32)[:, :1]
    place = jnp.sum(hotf * (rank + GROUP * first), axis=0, keepdims=True)
    live = jnp.sum(hotf, axis=0, keepdims=True) > 0
    place = jnp.where(live, place, -1.0).astype(i32)
    spot = (lax.broadcasted_iota(i32, (slots, tp), 0) == place).astype(f32).astype(bf16)
    t = lax.broadcasted_iota(i32, (1, tp), 1)
    row = lax.broadcasted_iota(i32, (8, tp), 0)
    data = jnp.where(row == 0, t // 128, jnp.where(row == 1, t % 128, jnp.where(row == 2, other_row, 1)))
    data = data.astype(f32).astype(bf16)
    got = lax.dot_general(data, spot, (((1,), (1,)), ((), ())), preferred_element_type=f32)
    there = got[3:4] > 0
    tile = jnp.where(there, got[0:1] * 128 + got[1:2], float(tiles)).astype(i32)
    other = jnp.where(there, got[2:3], 0.0).astype(i32)
    glanes = -(-(slots // GROUP) // 128) * 128
    ends = first + groups
    gi = lax.broadcasted_iota(i32, (nbp, glanes), 1).astype(f32)
    real = lax.broadcasted_iota(i32, (nbp, glanes), 0) < nb
    owner = jnp.sum(jnp.where(jnp.logical_and(ends <= gi, real), 1.0, 0.0), axis=0, keepdims=True).astype(i32)
    total = jnp.sum(groups, axis=0, keepdims=True).astype(i32)
    return tile, other, owner, total


def meta_kernel(tiles, nr, nc, slots_f, slots_b, rows_ref, cols_ref, count_ref,
                ft, fo, fb, bt, bo, bb, tot):
    tp = rows_ref.shape[1]
    live = lax.broadcasted_iota(i32, (1, tp), 1) < count_ref[0, 0]
    rows = rows_ref[...]
    cols = cols_ref[...]
    a, b, c, d = meta_one(jnp.where(live, rows, 4096), cols, tiles, nr, slots_f)
    ft[...], fo[...], fb[...] = a, b, c
    e, f, g, h = meta_one(jnp.where(live, cols, 4096), rows, tiles, nc, slots_b)
    bt[...], bo[...], bb[...] = e, f, g
    lane = lax.broadcasted_iota(i32, (1, 128), 1)
    tot[...] = jnp.where(lane == 0, d, h)


def up(n, m):
    return -(-n // m) * m


def make_meta(rows, cols, count, nr, nc):
    tiles = rows.shape[-1]
    tp = up(tiles, 128)
    pad = lambda v: jnp.pad(v.reshape(1, tiles), ((0, 0), (0, tp - tiles)))
    slots_f = up(tiles + 3 * min(nr, tiles), 512)
    slots_b = up(tiles + 3 * min(nc, tiles), 512)
    shapes = []
    for s in (slots_f, slots_b):
        shapes += [jax.ShapeDtypeStruct((1, s), i32)] * 2 + [jax.ShapeDtypeStruct((1, up(s // GROUP, 128)), i32)]
    shapes.append(jax.ShapeDtypeStruct((1, 128), i32))
    return pl.pallas_call(
        functools.partial(meta_kernel, tiles, nr, nc, slots_f, slots_b),
        out_shape=shapes,
        in_specs=[pl.BlockSpec(memory_space=pltpu.VMEM)] * 2 + [pl.BlockSpec(memory_space=pltpu.SMEM)],
        out_specs=[pl.BlockSpec(memory_space=pltpu.VMEM)] * 7,
        compiler_params=pltpu.CompilerParams(vmem_limit_bytes=48 << 20),
        name="meta",
    )(pad(rows), pad(cols), count.reshape(1, 1))


def swap_halves(m):
    return jnp.concatenate([m[:, 64:], m[:, :64]], axis=1)


def fwd_kernel(tiles, unroll, tot_ref, t_ref, o_ref, b_ref, m_ref, src_ref, out_ref, acc):
    low = lax.broadcasted_iota(i32, (32, 128), 1) < 64
    acc[...] = jnp.zeros_like(acc)

    def lhs_of(g):
        m = [m_ref[t_ref[0, g * 4 + k]] for k in range(4)]
        s = [swap_halves(v) for v in m]
        ev = [jnp.where(low, m[0], s[1]), jnp.where(low, m[2], s[3])]
        od = [jnp.where(low, s[0], m[1]), jnp.where(low, s[2], m[3])]
        return jnp.concatenate([jnp.concatenate(ev, axis=1), jnp.concatenate(od, axis=1)], axis=0)

    def body(i, _):
        prods = []
        for u in range(unroll):
            g = i * unroll + u
            rhs = jnp.concatenate([src_ref[o_ref[0, g * 4 + k]] for k in range(4)], axis=0)
            prods.append((b_ref[0, g], jnp.dot(lhs_of(g), rhs, preferred_element_type=f32)))
        for b, p in prods:
            acc[b] += p
        return 0

    lax.fori_loop(0, (tot_ref[0, 0] + unroll - 1) // unroll, body, 0)
    for s in range(out_ref.shape[0] // 8):
        out_ref[s * 8:s * 8 + 8] = acc[s * 8:s * 8 + 8].astype(bf16)


def bwd_kernel(tiles, unroll, tot_ref, t_ref, o_ref, b_ref, m_ref, src_ref, out_ref, acc):
    acc[...] = jnp.zeros_like(acc)

    def body(i, _):
        prods = []
        for u in range(unroll):
            g = i * unroll + u
            w = jnp.concatenate([m_ref[t_ref[0, g * 4 + k]] for k in range(4)], axis=0).T
            lhs = jnp.concatenate([w[:64], w[64:]], axis=1)
            src = [src_ref[o_ref[0, g * 4 + k]] for k in range(4)]
            rhs = jnp.concatenate([v[:32] for v in src] + [v[32:] for v in src], axis=0)
            prods.append((b_ref[0, g], jnp.dot(lhs, rhs, preferred_element_type=f32)))
        for b, p in prods:
            acc[b] += p
        return 0

    lax.fori_loop(0, (tot_ref[0, 1] + unroll - 1) // unroll, body, 0)
    for s in range(out_ref.shape[0] // 8):
        out_ref[s * 8:s * 8 + 8] = acc[s * 8:s * 8 + 8].astype(bf16)


def spmm(kernel, meta3, tot, m, src, nb, name, unroll=2):
    tiles = m.shape[0]
    width = src.shape[1]
    return pl.pallas_call(
        functools.partial(kernel, tiles, unroll),
        out_shape=jax.ShapeDtypeStruct((nb, BLOCK, width), bf16),
        in_specs=[pl.BlockSpec(memory_space=pltpu.SMEM)] * 4 + [pl.BlockSpec(memory_space=pltpu.VMEM)] * 2,
        out_specs=pl.BlockSpec(memory_space=pltpu.VMEM),
        scratch_shapes=[pltpu.VMEM((nb + 1, BLOCK, width), f32)],
        compiler_params=pltpu.CompilerParams(vmem_limit_bytes=56 << 20),
        name=name,
    )(tot, *meta3, m, src.reshape(-1, BLOCK, width))


def relayout(values):
    tiles = values.shape[2]
    m = values.reshape(tiles, 32, 128)
    return jnp.concatenate([m, jnp.zeros((1, 32, 128), bf16)], axis=0)


def activate(z):
    return jax.nn.gelu(z, approximate=True)


def per_device(features, weight, grad_out, tile_rows, tile_cols, tile_values, tile_counts):
    nodes_dev, width = features.shape
    nr = nodes_dev * lax.axis_size("col") // BLOCK
    nc = nodes_dev * lax.axis_size("row") // BLOCK
    source = lax.all_gather(features, "row", axis=0, tiled=True)
    *lists, tot = make_meta(tile_rows, tile_cols, tile_counts, nr, nc)
    m = relayout(tile_values)
    part = spmm(fwd_kernel, lists[:3], tot, m, source, nr, "spmm_fwd")
    hidden = lax.psum_scatter(part.reshape(-1, width), "col", scatter_dimension=0, tiled=True)
    hidden = hidden.reshape(-1, 2, BLOCK // 2, width).swapaxes(1, 2).reshape(nodes_dev, width)
    pre = jnp.dot(hidden, weight, preferred_element_type=f32)
    output = activate(pre).astype(bf16)
    grad_pre = jax.vjp(activate, pre)[1](grad_out.astype(f32))[0].astype(bf16)
    term = jnp.einsum("nd,ne->de", hidden, grad_pre, preferred_element_type=f32)
    grad_weight = lax.psum(term, ("row", "col"))
    grad_local = jnp.einsum("ne,de->nd", grad_pre, weight, preferred_element_type=f32).astype(bf16)
    grad_local = grad_local.reshape(-1, BLOCK // 2, 2, width).swapaxes(1, 2).reshape(nodes_dev, width)
    grad_hidden = lax.all_gather(grad_local, "col", axis=0, tiled=True)
    back = spmm(bwd_kernel, lists[3:], tot, m, grad_hidden, nc, "spmm_bwd")
    grad_feat = lax.psum_scatter(back.reshape(-1, width), "row", scatter_dimension=0, tiled=True)
    return output, grad_feat, grad_weight


def solution(mesh):
    placed = (
        P(("col", "row"), None),
        P(),
        P(("row", "col"), None),
        P("row", "col", None),
        P("row", "col", None),
        P("row", "col", None, None),
        P("row", "col"),
    )
    return jax.shard_map(
        per_device,
        mesh=mesh,
        in_specs=placed,
        out_specs=(P(("row", "col"), None), P(("col", "row"), None), P()),
        check_vma=False,
    )
```

```python
import functools
import jax, jax.numpy as jnp
from jax import lax
from jax.experimental import pallas as pl
from jax.experimental.pallas import tpu as pltpu
from jax.sharding import PartitionSpec as P

BLOCK = 64
GROUP = 4
f32, bf16, i32 = jnp.float32, jnp.bfloat16, jnp.int32


def meta_one(key_row, other_row, tiles, nb, slots):
    tp = key_row.shape[1]
    nbp = -(-nb // 128) * 128
    hot = lax.broadcasted_iota(i32, (nbp, tp), 0) == key_row
    hotf = hot.astype(f32)
    hotb = hotf.astype(bf16)
    count = jnp.sum(hotf, axis=1, keepdims=True)
    upper = (lax.broadcasted_iota(i32, (tp, tp), 0) < lax.broadcasted_iota(i32, (tp, tp), 1)).astype(f32).astype(bf16)
    rank = jnp.dot(hotb, upper, preferred_element_type=f32)
    groups = jnp.floor((count + (GROUP - 1)) * (1.0 / GROUP))
    lower = (lax.broadcasted_iota(i32, (nbp, nbp), 1) < lax.broadcasted_iota(i32, (nbp, nbp), 0)).astype(f32).astype(bf16)
    first = jnp.dot(lower, jnp.broadcast_to(groups, (nbp, 128)).astype(bf16), preferred_element_type=f32)[:, :1]
    place = jnp.sum(hotf * (rank + GROUP * first), axis=0, keepdims=True)
    live = jnp.sum(hotf, axis=0, keepdims=True) > 0
    place = jnp.where(live, place, -1.0).astype(i32)
    spot = (lax.broadcasted_iota(i32, (slots, tp), 0) == place).astype(f32).astype(bf16)
    t = lax.broadcasted_iota(i32, (1, tp), 1)
    row = lax.broadcasted_iota(i32, (8, tp), 0)
    data = jnp.where(row == 0, t // 128, jnp.where(row == 1, t % 128, jnp.where(row == 2, other_row, 1)))
    data = data.astype(f32).astype(bf16)
    got = lax.dot_general(data, spot, (((1,), (1,)), ((), ())), preferred_element_type=f32)
    there = got[3:4] > 0
    tile = jnp.where(there, got[0:1] * 128 + got[1:2], float(tiles)).astype(i32)
    other = jnp.where(there, got[2:3], 0.0).astype(i32)
    glanes = -(-(slots // GROUP) // 128) * 128
    ends = first + groups
    gi = lax.broadcasted_iota(i32, (nbp, glanes), 1).astype(f32)
    real = lax.broadcasted_iota(i32, (nbp, glanes), 0) < nb
    owner = jnp.sum(jnp.where(jnp.logical_and(ends <= gi, real), 1.0, 0.0), axis=0, keepdims=True).astype(i32)
    total = jnp.sum(groups, axis=0, keepdims=True).astype(i32)
    return tile, other, owner, total


def meta_kernel(tiles, nr, nc, slots_f, slots_b, rows_ref, cols_ref, count_ref,
                ft, fo, fb, bt, bo, bb, tot):
    tp = rows_ref.shape[1]
    live = lax.broadcasted_iota(i32, (1, tp), 1) < count_ref[0, 0]
    rows = rows_ref[...]
    cols = cols_ref[...]
    a, b, c, d = meta_one(jnp.where(live, rows, 4096), cols, tiles, nr, slots_f)
    ft[...], fo[...], fb[...] = a, b, c
    e, f, g, h = meta_one(jnp.where(live, cols, 4096), rows, tiles, nc, slots_b)
    bt[...], bo[...], bb[...] = e, f, g
    lane = lax.broadcasted_iota(i32, (1, 128), 1)
    tot[...] = jnp.where(lane == 0, d, h)


def up(n, m):
    return -(-n // m) * m


def make_meta(rows, cols, count, nr, nc):
    tiles = rows.shape[-1]
    tp = up(tiles, 128)
    pad = lambda v: jnp.pad(v.reshape(1, tiles), ((0, 0), (0, tp - tiles)))
    slots_f = up(tiles + 3 * min(nr, tiles), 512)
    slots_b = up(tiles + 3 * min(nc, tiles), 512)
    shapes = []
    for s in (slots_f, slots_b):
        shapes += [jax.ShapeDtypeStruct((1, s), i32)] * 2 + [jax.ShapeDtypeStruct((1, up(s // GROUP, 128)), i32)]
    shapes.append(jax.ShapeDtypeStruct((1, 128), i32))
    return pl.pallas_call(
        functools.partial(meta_kernel, tiles, nr, nc, slots_f, slots_b),
        out_shape=shapes,
        in_specs=[pl.BlockSpec(memory_space=pltpu.VMEM)] * 2 + [pl.BlockSpec(memory_space=pltpu.SMEM)],
        out_specs=[pl.BlockSpec(memory_space=pltpu.VMEM)] * 7,
        compiler_params=pltpu.CompilerParams(vmem_limit_bytes=48 << 20),
        name="meta",
    )(pad(rows), pad(cols), count.reshape(1, 1))


def swap_halves(m):
    return jnp.concatenate([m[:, 64:], m[:, :64]], axis=1)


def fwd_kernel(tiles, unroll, tot_ref, t_ref, o_ref, b_ref, m_ref, src_ref, out_ref, acc):
    low = lax.broadcasted_iota(i32, (32, 128), 1) < 64
    acc[...] = jnp.zeros_like(acc)

    def lhs_of(g):
        m = [m_ref[t_ref[0, g * 4 + k]] for k in range(4)]
        s = [swap_halves(v) for v in m]
        ev = [jnp.where(low, m[0], s[1]), jnp.where(low, m[2], s[3])]
        od = [jnp.where(low, s[0], m[1]), jnp.where(low, s[2], m[3])]
        return jnp.concatenate([jnp.concatenate(ev, axis=1), jnp.concatenate(od, axis=1)], axis=0)

    def body(i, _):
        prods = []
        for u in range(unroll):
            g = i * unroll + u
            rhs = jnp.concatenate([src_ref[o_ref[0, g * 4 + k]] for k in range(4)], axis=0)
            prods.append((b_ref[0, g], jnp.dot(lhs_of(g), rhs, preferred_element_type=f32)))
        for b, p in prods:
            acc[b] += p
        return 0

    lax.fori_loop(0, (tot_ref[0, 0] + unroll - 1) // unroll, body, 0)
    for s in range(out_ref.shape[0] // 8):
        out_ref[s * 8:s * 8 + 8] = acc[s * 8:s * 8 + 8].astype(bf16)


def bwd_kernel(tiles, unroll, tot_ref, t_ref, o_ref, b_ref, m_ref, src_ref, out_ref, acc):
    acc[...] = jnp.zeros_like(acc)

    def body(i, _):
        prods = []
        for u in range(unroll):
            g = i * unroll + u
            w = jnp.concatenate([m_ref[t_ref[0, g * 4 + k]] for k in range(4)], axis=0).T
            lhs = jnp.concatenate([w[:64], w[64:]], axis=1)
            src = [src_ref[o_ref[0, g * 4 + k]] for k in range(4)]
            rhs = jnp.concatenate([v[:32] for v in src] + [v[32:] for v in src], axis=0)
            prods.append((b_ref[0, g], jnp.dot(lhs, rhs, preferred_element_type=f32)))
        for b, p in prods:
            acc[b] += p
        return 0

    lax.fori_loop(0, (tot_ref[0, 1] + unroll - 1) // unroll, body, 0)
    for s in range(out_ref.shape[0] // 8):
        out_ref[s * 8:s * 8 + 8] = acc[s * 8:s * 8 + 8].astype(bf16)


def spmm(kernel, meta3, tot, m, src, nb, name, unroll=2):
    tiles = m.shape[0]
    width = src.shape[1]
    return pl.pallas_call(
        functools.partial(kernel, tiles, unroll),
        out_shape=jax.ShapeDtypeStruct((nb, BLOCK, width), bf16),
        in_specs=[pl.BlockSpec(memory_space=pltpu.SMEM)] * 4 + [pl.BlockSpec(memory_space=pltpu.VMEM)] * 2,
        out_specs=pl.BlockSpec(memory_space=pltpu.VMEM),
        scratch_shapes=[pltpu.VMEM((nb + 1, BLOCK, width), f32)],
        compiler_params=pltpu.CompilerParams(vmem_limit_bytes=56 << 20),
        name=name,
    )(tot, *meta3, m, src.reshape(-1, BLOCK, width))


def relayout(values):
    tiles = values.shape[2]
    m = values.reshape(tiles, 32, 128)
    return jnp.concatenate([m, jnp.zeros((1, 32, 128), bf16)], axis=0)

MESH = pl.DeviceIdType.MESH
RING = 4
ANY = pl.ANY
VM = pltpu.VMEM


class Wire:
    def __init__(self, send_sem, recv_sem):
        self.send_sem, self.recv_sem = send_sem, recv_sem
        self.ids, self.sent = {}, []

    def _sems(self, key):
        n = self.ids.setdefault(key, len(self.ids))
        assert n < self.send_sem.shape[0]
        return dict(send_sem=self.send_sem.at[n], recv_sem=self.recv_sem.at[n])

    def push(self, key, src, dst, dev):
        copy = pltpu.make_async_remote_copy(
            src_ref=src, dst_ref=dst, device_id=dev, device_id_type=MESH, **self._sems(key))
        copy.start()
        self.sent.append(copy)

    def take(self, key, dst, dev):
        pltpu.make_async_remote_copy(
            src_ref=dst, dst_ref=dst, device_id=dev, device_id_type=MESH, **self._sems(key)).wait_recv()

    def drain(self):
        for copy in self.sent:
            copy.wait_send()


def barrier(devs):
    sem = pltpu.get_barrier_semaphore()
    for dev in devs:
        pl.semaphore_signal(sem, inc=1, device_id=dev, device_id_type=MESH)
    pl.semaphore_wait(sem, len(devs))


def row_place():
    r = lax.axis_index("row")
    pair, ring, core = r // (2 * RING), (r // 2) % RING, r % 2

    def blk(p, d, s=0):
        return (pair + p) % 2 * (2 * RING) + (ring + d) % RING * 2 + (core + s) % 2

    return blk, (lambda p, d, s=0: {"row": blk(p, d, s)}), core


def col_place():
    c = lax.axis_index("col")
    pair, ring = c // RING, c % RING

    def blk(p, d):
        return (pair + p) % 2 * RING + (ring + d) % RING

    return blk, (lambda p, d: {"col": blk(p, d)})


def gather_kernel(nchunk, first_a, feat, out, send_sem, recv_sem, own_sem):
    blk, dev, _ = row_place()
    wire = Wire(send_sem, recv_sem)
    rows = feat.shape[0] // nchunk
    kind_a = [k for k in range(nchunk) if k < first_a]
    kind_b = [k for k in range(nchunk) if k >= first_a]
    to = {"R": dev(0, 1), "L": dev(0, -1), "Y": dev(1, 0), "S": dev(0, 0, 1)}
    barrier(list(to.values()))
    own = pltpu.make_async_copy(feat, out.at[blk(0, 0)], own_sem)
    own.start()

    def slot(p, d, s, k):
        return out.at[blk(p, d, s), pl.ds(k * rows, rows)]

    def push(way, p, d, k):
        src = feat.at[pl.ds(k * rows, rows)] if (p, d) == (0, 0) else slot(p, d, 0, k)
        wire.push((way, p, d, k), src, slot(p, d, 0, k), to[way])

    def take(way, p, d, k):
        if way == "S":
            wire.take((way, p, d, k), slot(p, d, 1, k), to["S"])
            return
        q, e = {"R": (p, d - 1), "L": (p, d + 1), "Y": (1 - p, d)}[way]
        wire.take((way, p, d, k), slot(q, e, 0, k), to["S"])
        a = k in kind_a
        if way == "Y":
            if not a:
                push("R", q, e, k)
                push("L", q, e, k)
        else:
            if a:
                push("Y", q, e, k)
            if abs(e) == 1 and (k % 2 == 0) == (way == "R"):
                push(way, q, e, k)
        push("S", q, e, k)

    for k in kind_b + kind_a:
        push("Y", 0, 0, k)
        push("R", 0, 0, k)
        push("L", 0, 0, k)
    for k in kind_b + kind_a:
        push("S", 0, 0, k)
    for k in kind_b:
        take("Y", 0, 0, k)
    for k in kind_a:
        take("R", 0, 0, k)
        take("L", 0, 0, k)
    for k in kind_a:
        take("Y", 0, 0, k)
    for k in kind_b:
        take("R", 0, 0, k)
        take("L", 0, 0, k)
    for k in kind_a:
        take(*(("R", 0, -1, k) if k % 2 == 0 else ("L", 0, 1, k)))
    for k in kind_b:
        take("R", 1, 0, k)
        take("L", 1, 0, k)
    for k in kind_a:
        take("Y", 0, -1, k)
        take("Y", 0, 1, k)
    for p in (0, 1):
        for k in kind_b:
            take(*(("R", p, -1, k) if k % 2 == 0 else ("L", p, 1, k)))
    for k in kind_a:
        take("Y", 0, -2 if k % 2 == 0 else 2, k)
    for (way, p, d, k) in [key for key in wire.ids if key[0] == "S"]:
        take("S", p, d, k)
    own.wait()
    wire.drain()


def gather_rows(features, nchunk=4, first_a=2, cid=1):
    n = 4 * RING
    return pl.pallas_call(
        functools.partial(gather_kernel, nchunk, first_a),
        out_shape=jax.ShapeDtypeStruct((n,) + features.shape, features.dtype),
        in_specs=[pl.BlockSpec(memory_space=VM)],
        out_specs=pl.BlockSpec(memory_space=ANY),
        scratch_shapes=[pltpu.SemaphoreType.DMA((128,)), pltpu.SemaphoreType.DMA((128,)), pltpu.SemaphoreType.DMA],
        compiler_params=pltpu.CompilerParams(collective_id=cid, has_side_effects=True, vmem_limit_bytes=48 << 20),
        name="gather_rows",
    )(features)


def gelu_both(z):
    c, a = 0.7978845608, 0.044715
    z2 = z * z
    t = jnp.tanh(c * (z + a * z * z2))
    half = 0.5 * (1.0 + t)
    slope = half + 0.5 * z * (1.0 - t * t) * (c * (1.0 + 3.0 * a * z2))
    return z * half, slope


def middle_kernel(nchunk, part, weight, gout, out, gh, gw,
                  opp_in, t_out, in_r, in_l, s_out, y_in, gl, send_sem, recv_sem, own_sem):
    blk, dev = col_place()
    wire = Wire(send_sem, recv_sem)
    rows = gout.shape[0] // nchunk
    to = {"R": dev(0, 1), "L": dev(0, -1), "Y": dev(1, 0)}
    barrier(list(to.values()))
    cut = lambda k: pl.ds(k * rows, rows)
    f = lambda v: v.astype(f32)
    chunks = range(nchunk)
    way_of = lambda k: "R" if k % 2 == 0 else "L"
    side = {"R": 1, "L": -1}
    arrive = {"R": in_r, "L": in_l}
    other = {"R": "L", "L": "R"}

    for k in chunks:
        for p in (1, 0):
            wire.push(("opp", p, k), part.at[blk(p, 2), cut(k)], opp_in.at[p, cut(k)], to[way_of(k)])
    for k in chunks:
        w = other[way_of(k)]
        for p in (1, 0):
            wire.push((w, p, k), part.at[blk(p, side[w]), cut(k)], arrive[w].at[p, cut(k)], to[w])

    def stage2(k):
        w = way_of(k)
        for p in (1, 0):
            wire.take(("opp", p, k), opp_in.at[p, cut(k)], to["Y"])
            t_out[p, cut(k)] = (f(part[blk(p, side[w]), cut(k)]) + f(opp_in[p, cut(k)])).astype(bf16)
            wire.push((w, p, k), t_out.at[p, cut(k)], arrive[w].at[p, cut(k)], to[w])

    def ring_sum(p, k):
        for w in "RL":
            wire.take((w, p, k), arrive[w].at[p, cut(k)], to["Y"])
        return f(part[blk(p, 0), cut(k)]) + f(in_r[p, cut(k)]) + f(in_l[p, cut(k)])

    def stage3(k):
        s_out[cut(k)] = ring_sum(1, k).astype(bf16)
        wire.push(("y", k), s_out.at[cut(k)], y_in.at[cut(k)], to["Y"])

    i0 = lax.broadcasted_iota(i32, (rows, rows), 0)
    i1 = lax.broadcasted_iota(i32, (rows, rows), 1)
    inside = i0 % BLOCK
    node = i0 - inside + jnp.where(inside < BLOCK // 2, 2 * inside, 2 * inside - (BLOCK - 1))
    order = (node == i1).astype(f32).astype(bf16)
    locals_ = []

    def stage4(k):
        total = ring_sum(0, k)
        wire.take(("y", k), y_in.at[cut(k)], to["Y"])
        hidden = (total + f(y_in[cut(k)])).astype(bf16)
        w = weight[...]
        pre = jnp.dot(hidden, w, preferred_element_type=f32)
        go = jnp.dot(order, gout[cut(k)], preferred_element_type=f32)
        act, slope = gelu_both(pre)
        gp = (go * slope).astype(bf16)
        gl[cut(k)] = lax.dot_general(gp, w, (((1,), (1,)), ((), ())), preferred_element_type=f32).astype(bf16)
        for way in "YRL":
            wire.push(("g" + way, 0, 0, k), gl.at[cut(k)], gh.at[blk(0, 0), cut(k)], to[way])
        own = pltpu.make_async_copy(gl.at[cut(k)], gh.at[blk(0, 0), cut(k)], own_sem.at[k])
        own.start()
        locals_.append(own)
        out[cut(k)] = lax.dot_general(order, act.astype(bf16), (((0,), (0,)), ((), ())),
                                      preferred_element_type=f32).astype(bf16)
        term = lax.dot_general(hidden, gp, (((0,), (0,)), ((), ())), preferred_element_type=f32)
        if k == 0:
            gw[...] = term
        else:
            gw[...] += term

    def stage5(k):
        spot = gh.at[blk(1, 0), cut(k)]
        wire.take(("gY", 0, 0, k), spot, to["Y"])
        for way in "RL":
            wire.push(("g" + way, 1, 0, k), spot, spot, to[way])

    def stage6(k):
        for p in (0, 1):
            for way in "RL":
                d = -side[way]
                spot = gh.at[blk(p, d), cut(k)]
                wire.take(("g" + way, p, 0, k), spot, to["Y"])
                if way == way_of(k):
                    wire.push(("g" + way, p, 1, k), spot, spot, to[way])

    def stage7(k):
        for p in (0, 1):
            wire.take(("g" + way_of(k), p, 1, k), gh.at[blk(p, 2), cut(k)], to["Y"])

    for k in chunks:
        stage2(k)
    stages = [stage3, stage4, stage5, stage6, stage7]
    for tick in range(nchunk + len(stages) - 1):
        for s, stage in enumerate(stages):
            if 0 <= tick - s < nchunk:
                stage(tick - s)
    for own in locals_:
        own.wait()
    wire.drain()


def middle(part, weight, gout, nchunk=4, cid=2):
    rows, width = gout.shape
    n = part.shape[0]
    piece = lambda *lead: pltpu.VMEM(lead + (rows, width), bf16)
    return pl.pallas_call(
        functools.partial(middle_kernel, nchunk),
        out_shape=[jax.ShapeDtypeStruct((rows, width), bf16),
                   jax.ShapeDtypeStruct((n, rows, width), bf16),
                   jax.ShapeDtypeStruct((width, width), f32)],
        in_specs=[pl.BlockSpec(memory_space=VM)] * 3,
        out_specs=[pl.BlockSpec(memory_space=VM), pl.BlockSpec(memory_space=ANY), pl.BlockSpec(memory_space=VM)],
        scratch_shapes=[piece(2), piece(2), piece(2), piece(2), piece(), piece(), piece(),
                        pltpu.SemaphoreType.DMA((128,)), pltpu.SemaphoreType.DMA((128,)),
                        pltpu.SemaphoreType.DMA((nchunk,))],
        compiler_params=pltpu.CompilerParams(collective_id=cid, has_side_effects=True, vmem_limit_bytes=48 << 20),
        name="middle",
    )(part, weight, gout)


def last_kernel(nchunk, part, term, out, gw,
                sib_in, opp_out, opp_in, d_out, t_out, in_r, in_l, s_out, y_in,
                w_sib, w_half, w_row, w_col, w_sum, w_full, send_sem, recv_sem):
    blk, dev, core = row_place()
    cblk, cdev = col_place()
    wire = Wire(send_sem, recv_sem)
    rows = out.shape[0] // nchunk
    to = {"R": dev(0, 1), "L": dev(0, -1), "Y": dev(1, 0), "S": dev(0, 0, 1)}
    peers = [(p, d) for p in (0, 1) for d in range(RING) if (p, d) != (0, 0)]
    barrier([to["S"]] + [dev(p, d) for p, d in peers] + [cdev(p, d) for p, d in peers])
    cut = lambda k: pl.ds(k * rows, rows)
    f = lambda v: v.astype(f32)
    chunks = range(nchunk)
    way_of = lambda k: "R" if k % 2 == 0 else "L"
    side = {"R": 1, "L": -1}
    arrive = {"R": in_r, "L": in_l}
    other = {"R": "L", "L": "R"}
    rel = lambda p, d: p * RING + d % RING

    half = term.shape[0] // 2
    ninth = half // (2 * RING)
    hd = lambda c: pl.ds(pl.multiple_of(c * half, half), half)
    seat = lambda p, d: blk(p, d) // 2
    sd = lambda j: pl.ds(pl.multiple_of(j * ninth, ninth), ninth)
    wire.push("w0", term.at[hd(1 - core)], w_sib, to["S"])

    def sib(p, d, k):
        wire.push(("s", rel(p, d), k), part.at[blk(p, d, 1), cut(k)], sib_in.at[rel(p, d), cut(k)], to["S"])

    for k in chunks:
        for p in (1, 0):
            sib(p, 2, k)
    for k in chunks:
        for p in (1, 0):
            sib(p, side[other[way_of(k)]], k)
    for k in chunks:
        for p in (1, 0):
            sib(p, side[way_of(k)], k)
    for k in chunks:
        for p in (1, 0):
            sib(p, 0, k)

    def both(p, d, k):
        wire.take(("s", rel(p, d), k), sib_in.at[rel(p, d), cut(k)], to["S"])
        return f(part[blk(p, d), cut(k)]) + f(sib_in[rel(p, d), cut(k)])

    for k in chunks:
        for p in (1, 0):
            opp_out[p, cut(k)] = both(p, 2, k).astype(bf16)
            wire.push(("opp", p, k), opp_out.at[p, cut(k)], opp_in.at[p, cut(k)], to[way_of(k)])
    for k in chunks:
        w = other[way_of(k)]
        for p in (1, 0):
            d_out[p, cut(k)] = both(p, side[w], k).astype(bf16)
            wire.push((w, p, k), d_out.at[p, cut(k)], arrive[w].at[p, cut(k)], to[w])

    wire.take("w0", w_sib, to["S"])
    w_half[...] = term[hd(core)] + w_sib[...]
    for i, (p, d) in enumerate(peers):
        wire.push(("w1", i), w_half.at[sd(seat(p, d))], w_row.at[i], dev(p, d))

    def stage2(k):
        w = way_of(k)
        for p in (1, 0):
            base = both(p, side[w], k)
            wire.take(("opp", p, k), opp_in.at[p, cut(k)], to["Y"])
            t_out[p, cut(k)] = (base + f(opp_in[p, cut(k)])).astype(bf16)
            wire.push((w, p, k), t_out.at[p, cut(k)], arrive[w].at[p, cut(k)], to[w])

    def ring_sum(p, k):
        base = both(p, 0, k)
        for w in "RL":
            wire.take((w, p, k), arrive[w].at[p, cut(k)], to["Y"])
        return base + f(in_r[p, cut(k)]) + f(in_l[p, cut(k)])

    def stage3(k):
        s_out[cut(k)] = ring_sum(1, k).astype(bf16)
        wire.push(("y", k), s_out.at[cut(k)], y_in.at[cut(k)], to["Y"])

    def stage4(k):
        total = ring_sum(0, k)
        wire.take(("y", k), y_in.at[cut(k)], to["Y"])
        out[cut(k)] = (total + f(y_in[cut(k)])).astype(bf16)

    for k in chunks:
        stage2(k)
        if k == 1:
            mine = w_half[sd(seat(0, 0))]
            for i, (p, d) in enumerate(peers):
                wire.take(("w1", i), w_row.at[i], to["Y"])
                mine = mine + w_row[i]
            w_sum[...] = mine
            here = cblk(0, 0)
            w_col[here] = mine
            for i, (p, d) in enumerate(peers):
                wire.push(("w2", i), w_sum, w_col.at[here], cdev(p, d))
    for i, (p, d) in enumerate(peers):
        wire.take(("w2", i), w_col.at[cblk(p, -d)], to["Y"])
    total = w_col[0]
    for i in range(1, 2 * RING):
        total = total + w_col[i]
    spot = lambda p, d: pl.ds(pl.multiple_of(core * half + seat(p, d) * ninth, ninth), ninth)
    w_full[spot(0, 0)] = total
    for i, (p, d) in enumerate(peers):
        wire.push(("w3", i), w_full.at[spot(0, 0)], w_full.at[spot(0, 0)], dev(p, d))
    stages = [stage3, stage4]
    for tick in range(nchunk + len(stages) - 1):
        for s, stage in enumerate(stages):
            if 0 <= tick - s < nchunk:
                stage(tick - s)
        if tick == 0:
            for i, (p, d) in enumerate(peers):
                wire.take(("w3", i), w_full.at[spot(p, -d)], to["Y"])
            wire.push("w4", w_full.at[hd(core)], w_full.at[hd(core)], to["S"])
    wire.take("w4", w_full.at[hd(1 - core)], to["S"])
    gw[...] = w_full[...]
    wire.drain()


def last(part, term, nchunk=4, cid=3):
    n, rows, width = part.shape
    piece = lambda *lead: pltpu.VMEM(lead + (rows, width), bf16)
    wrows = term.shape[0]
    wf = lambda *lead: pltpu.VMEM(lead + (term.shape[1],), f32)
    nine = wrows // (4 * RING)
    return pl.pallas_call(
        functools.partial(last_kernel, nchunk),
        out_shape=[jax.ShapeDtypeStruct((rows, width), bf16), jax.ShapeDtypeStruct(term.shape, f32)],
        in_specs=[pl.BlockSpec(memory_space=VM)] * 2,
        out_specs=[pl.BlockSpec(memory_space=VM)] * 2,
        scratch_shapes=[piece(n // 2), piece(2), piece(2), piece(2), piece(2), piece(2), piece(2), piece(), piece(),
                        wf(wrows // 2), wf(wrows // 2), wf(2 * RING - 1, nine), wf(2 * RING, nine), wf(nine), wf(wrows),
                        pltpu.SemaphoreType.DMA((160,)), pltpu.SemaphoreType.DMA((160,))],
        compiler_params=pltpu.CompilerParams(collective_id=cid, has_side_effects=True, vmem_limit_bytes=48 << 20),
        name="last",
    )(part, term)


def per_device(features, weight, grad_out, tile_rows, tile_cols, tile_values, tile_counts):
    nodes_dev, width = features.shape
    nr = nodes_dev * lax.axis_size("col") // BLOCK
    nc = nodes_dev * lax.axis_size("row") // BLOCK
    *lists, tot = make_meta(tile_rows, tile_cols, tile_counts, nr, nc)
    m = relayout(tile_values)
    source = gather_rows(features)
    part = spmm(fwd_kernel, lists[:3], tot, m, source.reshape(-1, width), nr, "spmm_fwd")
    output, grad_hidden, term = middle(part.reshape(-1, nodes_dev, width), weight, grad_out)
    back = spmm(bwd_kernel, lists[3:], tot, m, grad_hidden.reshape(-1, width), nc, "spmm_bwd")
    grad_feat, grad_weight = last(back.reshape(-1, nodes_dev, width), term)
    return output, grad_feat, grad_weight


def solution(mesh):
    placed = (
        P(("col", "row"), None),
        P(),
        P(("row", "col"), None),
        P("row", "col", None),
        P("row", "col", None),
        P("row", "col", None, None),
        P("row", "col"),
    )
    return jax.shard_map(
        per_device,
        mesh=mesh,
        in_specs=placed,
        out_specs=(P(("row", "col"), None), P(("col", "row"), None), P()),
        check_vma=False,
    )
```

```python
import functools
import jax, jax.numpy as jnp
from jax import lax
from jax.experimental import pallas as pl
from jax.experimental.pallas import tpu as pltpu
from jax.sharding import PartitionSpec as P

BLOCK = 64
GROUP = 4
f32, bf16, i32 = jnp.float32, jnp.bfloat16, jnp.int32


def meta_one(key_row, other_row, tiles, nb, slots):
    tp = key_row.shape[1]
    nbp = -(-nb // 128) * 128
    hot = lax.broadcasted_iota(i32, (nbp, tp), 0) == key_row
    hotf = hot.astype(f32)
    hotb = hotf.astype(bf16)
    count = jnp.sum(hotf, axis=1, keepdims=True)
    upper = (lax.broadcasted_iota(i32, (tp, tp), 0) < lax.broadcasted_iota(i32, (tp, tp), 1)).astype(f32).astype(bf16)
    rank = jnp.dot(hotb, upper, preferred_element_type=f32)
    groups = jnp.floor((count + (GROUP - 1)) * (1.0 / GROUP))
    lower = (lax.broadcasted_iota(i32, (nbp, nbp), 1) < lax.broadcasted_iota(i32, (nbp, nbp), 0)).astype(f32).astype(bf16)
    first = jnp.dot(lower, jnp.broadcast_to(groups, (nbp, 128)).astype(bf16), preferred_element_type=f32)[:, :1]
    place = jnp.sum(hotf * (rank + GROUP * first), axis=0, keepdims=True)
    live = jnp.sum(hotf, axis=0, keepdims=True) > 0
    place = jnp.where(live, place, -1.0).astype(i32)
    spot = (lax.broadcasted_iota(i32, (slots, tp), 0) == place).astype(f32).astype(bf16)
    t = lax.broadcasted_iota(i32, (1, tp), 1)
    row = lax.broadcasted_iota(i32, (8, tp), 0)
    data = jnp.where(row == 0, t // 128, jnp.where(row == 1, t % 128, jnp.where(row == 2, other_row, 1)))
    data = data.astype(f32).astype(bf16)
    got = lax.dot_general(data, spot, (((1,), (1,)), ((), ())), preferred_element_type=f32)
    there = got[3:4] > 0
    tile = jnp.where(there, got[0:1] * 128 + got[1:2], float(tiles)).astype(i32)
    other = jnp.where(there, got[2:3], 0.0).astype(i32)
    glanes = -(-(slots // GROUP) // 128) * 128
    ends = first + groups
    gi = lax.broadcasted_iota(i32, (nbp, glanes), 1).astype(f32)
    real = lax.broadcasted_iota(i32, (nbp, glanes), 0) < nb
    owner = jnp.sum(jnp.where(jnp.logical_and(ends <= gi, real), 1.0, 0.0), axis=0, keepdims=True).astype(i32)
    total = jnp.sum(groups, axis=0, keepdims=True).astype(i32)
    return tile, other, owner, total


def meta_kernel(tiles, nr, nc, slots_f, slots_b, rows_ref, cols_ref, count_ref,
                ft, fo, fb, bt, bo, bb, tot):
    tp = rows_ref.shape[1]
    live = lax.broadcasted_iota(i32, (1, tp), 1) < count_ref[0, 0]
    rows = rows_ref[...]
    cols = cols_ref[...]
    a, b, c, d = meta_one(jnp.where(live, rows, 4096), cols, tiles, nr, slots_f)
    ft[...], fo[...], fb[...] = a, b, c
    e, f, g, h = meta_one(jnp.where(live, cols, 4096), rows, tiles, nc, slots_b)
    bt[...], bo[...], bb[...] = e, f, g
    lane = lax.broadcasted_iota(i32, (1, 128), 1)
    tot[...] = jnp.where(lane == 0, d, h)


def up(n, m):
    return -(-n // m) * m


def make_meta(rows, cols, count, nr, nc):
    tiles = rows.shape[-1]
    tp = up(tiles, 128)
    pad = lambda v: jnp.pad(v.reshape(1, tiles), ((0, 0), (0, tp - tiles)))
    slots_f = up(tiles + 3 * min(nr, tiles), 512)
    slots_b = up(tiles + 3 * min(nc, tiles), 512)
    shapes = []
    for s in (slots_f, slots_b):
        shapes += [jax.ShapeDtypeStruct((1, s), i32)] * 2 + [jax.ShapeDtypeStruct((1, up(s // GROUP, 128)), i32)]
    shapes.append(jax.ShapeDtypeStruct((1, 128), i32))
    return pl.pallas_call(
        functools.partial(meta_kernel, tiles, nr, nc, slots_f, slots_b),
        out_shape=shapes,
        in_specs=[pl.BlockSpec(memory_space=pltpu.VMEM)] * 2 + [pl.BlockSpec(memory_space=pltpu.SMEM)],
        out_specs=[pl.BlockSpec(memory_space=pltpu.VMEM)] * 7,
        compiler_params=pltpu.CompilerParams(vmem_limit_bytes=48 << 20),
        name="meta",
    )(pad(rows), pad(cols), count.reshape(1, 1))


def swap_halves(m):
    return jnp.concatenate([m[:, 64:], m[:, :64]], axis=1)


def fwd_kernel(tiles, unroll, tot_ref, t_ref, o_ref, b_ref, m_ref, src_ref, out_ref, acc):
    low = lax.broadcasted_iota(i32, (32, 128), 1) < 64
    acc[...] = jnp.zeros_like(acc)

    def lhs_of(g):
        m = [m_ref[t_ref[0, g * 4 + k]] for k in range(4)]
        s = [swap_halves(v) for v in m]
        ev = [jnp.where(low, m[0], s[1]), jnp.where(low, m[2], s[3])]
        od = [jnp.where(low, s[0], m[1]), jnp.where(low, s[2], m[3])]
        return jnp.concatenate([jnp.concatenate(ev, axis=1), jnp.concatenate(od, axis=1)], axis=0)

    def body(i, _):
        prods = []
        for u in range(unroll):
            g = i * unroll + u
            rhs = jnp.concatenate([src_ref[o_ref[0, g * 4 + k]] for k in range(4)], axis=0)
            prods.append((b_ref[0, g], jnp.dot(lhs_of(g), rhs, preferred_element_type=f32)))
        for b, p in prods:
            acc[b] += p
        return 0

    lax.fori_loop(0, (tot_ref[0, 0] + unroll - 1) // unroll, body, 0)
    for s in range(out_ref.shape[0] // 8):
        out_ref[s * 8:s * 8 + 8] = acc[s * 8:s * 8 + 8].astype(bf16)


def bwd_kernel(tiles, unroll, tot_ref, t_ref, o_ref, b_ref, m_ref, src_ref, out_ref, acc):
    acc[...] = jnp.zeros_like(acc)

    def body(i, _):
        prods = []
        for u in range(unroll):
            g = i * unroll + u
            w = jnp.concatenate([m_ref[t_ref[0, g * 4 + k]] for k in range(4)], axis=0).T
            lhs = jnp.concatenate([w[:64], w[64:]], axis=1)
            src = [src_ref[o_ref[0, g * 4 + k]] for k in range(4)]
            rhs = jnp.concatenate([v[:32] for v in src] + [v[32:] for v in src], axis=0)
            prods.append((b_ref[0, g], jnp.dot(lhs, rhs, preferred_element_type=f32)))
        for b, p in prods:
            acc[b] += p
        return 0

    lax.fori_loop(0, (tot_ref[0, 1] + unroll - 1) // unroll, body, 0)
    for s in range(out_ref.shape[0] // 8):
        out_ref[s * 8:s * 8 + 8] = acc[s * 8:s * 8 + 8].astype(bf16)


def spmm(kernel, meta3, tot, m, src, nb, name, unroll=16):
    tiles = m.shape[0]
    width = src.shape[1]
    return pl.pallas_call(
        functools.partial(kernel, tiles, unroll),
        out_shape=jax.ShapeDtypeStruct((nb, BLOCK, width), bf16),
        in_specs=[pl.BlockSpec(memory_space=pltpu.SMEM)] * 4 + [pl.BlockSpec(memory_space=pltpu.VMEM)] * 2,
        out_specs=pl.BlockSpec(memory_space=pltpu.VMEM),
        scratch_shapes=[pltpu.VMEM((nb + 1, BLOCK, width), f32)],
        compiler_params=pltpu.CompilerParams(vmem_limit_bytes=56 << 20),
        name=name,
    )(tot, *meta3, m, src.reshape(-1, BLOCK, width))


def relayout(values):
    tiles = values.shape[2]
    m = values.reshape(tiles, 32, 128)
    return jnp.concatenate([m, jnp.zeros((1, 32, 128), bf16)], axis=0)

MESH = pl.DeviceIdType.MESH
RING = 4
ANY = pl.ANY
VM = pltpu.VMEM


class Wire:
    def __init__(self, send_sem, recv_sem):
        self.send_sem, self.recv_sem = send_sem, recv_sem
        self.ids, self.sent = {}, []

    def _sems(self, key):
        n = self.ids.setdefault(key, len(self.ids))
        assert n < self.send_sem.shape[0]
        return dict(send_sem=self.send_sem.at[n], recv_sem=self.recv_sem.at[n])

    def push(self, key, src, dst, dev):
        copy = pltpu.make_async_remote_copy(
            src_ref=src, dst_ref=dst, device_id=dev, device_id_type=MESH, **self._sems(key))
        copy.start()
        self.sent.append(copy)

    def take(self, key, dst, dev):
        pltpu.make_async_remote_copy(
            src_ref=dst, dst_ref=dst, device_id=dev, device_id_type=MESH, **self._sems(key)).wait_recv()

    def drain(self):
        for copy in self.sent:
            copy.wait_send()


def barrier(devs):
    sem = pltpu.get_barrier_semaphore()
    for dev in devs:
        pl.semaphore_signal(sem, inc=1, device_id=dev, device_id_type=MESH)
    pl.semaphore_wait(sem, len(devs))


def row_place():
    r = lax.axis_index("row")
    pair, ring, core = r // (2 * RING), (r // 2) % RING, r % 2

    def blk(p, d, s=0):
        return (pair + p) % 2 * (2 * RING) + (ring + d) % RING * 2 + (core + s) % 2

    return blk, (lambda p, d, s=0: {"row": blk(p, d, s)}), core


def col_place():
    c = lax.axis_index("col")
    pair, ring = c // RING, c % RING

    def blk(p, d):
        return (pair + p) % 2 * RING + (ring + d) % RING

    return blk, (lambda p, d: {"col": blk(p, d)})


def gather_kernel(nchunk, first_a, feat, values, out, m_out, send_sem, recv_sem, own_sem):
    blk, dev, _ = row_place()
    wire = Wire(send_sem, recv_sem)
    rows = feat.shape[0] // nchunk
    kind_a = [k for k in range(nchunk) if k < first_a]
    kind_b = [k for k in range(nchunk) if k >= first_a]
    to = {"R": dev(0, 1), "L": dev(0, -1), "Y": dev(1, 0), "S": dev(0, 0, 1)}
    barrier(list(to.values()))
    own = pltpu.make_async_copy(feat, out.at[blk(0, 0)], own_sem)
    own.start()

    def slot(p, d, s, k):
        return out.at[blk(p, d, s), pl.ds(k * rows, rows)]

    def push(way, p, d, k):
        src = feat.at[pl.ds(k * rows, rows)] if (p, d) == (0, 0) else slot(p, d, 0, k)
        wire.push((way, p, d, k), src, slot(p, d, 0, k), to[way])

    def take(way, p, d, k):
        if way == "S":
            wire.take((way, p, d, k), slot(p, d, 1, k), to["S"])
            return
        q, e = {"R": (p, d - 1), "L": (p, d + 1), "Y": (1 - p, d)}[way]
        wire.take((way, p, d, k), slot(q, e, 0, k), to["S"])
        a = k in kind_a
        if way == "Y":
            if not a:
                push("R", q, e, k)
                push("L", q, e, k)
        else:
            if a:
                push("Y", q, e, k)
            if abs(e) == 1 and (k % 2 == 0) == (way == "R"):
                push(way, q, e, k)
        push("S", q, e, k)

    for k in kind_b + kind_a:
        push("Y", 0, 0, k)
        push("R", 0, 0, k)
        push("L", 0, 0, k)
    for k in kind_b + kind_a:
        push("S", 0, 0, k)
    tiles = values.shape[0]

    for s in range(0, tiles, 16):
        m_out[s:s + 16] = values[s:s + 16].reshape((16,) + m_out.shape[1:])
    m_out[tiles:] = jnp.zeros((1,) + m_out.shape[1:], bf16)
    for k in kind_b:
        take("Y", 0, 0, k)
    for k in kind_a:
        take("R", 0, 0, k)
        take("L", 0, 0, k)
    for k in kind_a:
        take("Y", 0, 0, k)
    for k in kind_b:
        take("R", 0, 0, k)
        take("L", 0, 0, k)
    for k in kind_a:
        take(*(("R", 0, -1, k) if k % 2 == 0 else ("L", 0, 1, k)))
    for k in kind_b:
        take("R", 1, 0, k)
        take("L", 1, 0, k)
    for k in kind_a:
        take("Y", 0, -1, k)
        take("Y", 0, 1, k)
    for p in (0, 1):
        for k in kind_b:
            take(*(("R", p, -1, k) if k % 2 == 0 else ("L", p, 1, k)))
    for k in kind_a:
        take("Y", 0, -2 if k % 2 == 0 else 2, k)
    for (way, p, d, k) in [key for key in wire.ids if key[0] == "S"]:
        take("S", p, d, k)
    own.wait()
    wire.drain()


def gather_rows(features, values, nchunk=4, first_a=2, cid=1):
    n = 4 * RING
    return pl.pallas_call(
        functools.partial(gather_kernel, nchunk, first_a),
        out_shape=[jax.ShapeDtypeStruct((n,) + features.shape, features.dtype),
                   jax.ShapeDtypeStruct((values.shape[0] + 1, BLOCK // 2, 2 * BLOCK), bf16)],
        in_specs=[pl.BlockSpec(memory_space=VM)] * 2,
        out_specs=[pl.BlockSpec(memory_space=ANY), pl.BlockSpec(memory_space=VM)],
        scratch_shapes=[pltpu.SemaphoreType.DMA((128,)), pltpu.SemaphoreType.DMA((128,)), pltpu.SemaphoreType.DMA],
        compiler_params=pltpu.CompilerParams(collective_id=cid, has_side_effects=True, vmem_limit_bytes=48 << 20),
        name="gather_rows",
    )(features, values)


def gelu_both(z):
    c, a = 0.7978845608, 0.044715
    z2 = z * z
    t = jnp.tanh(c * (z + a * z * z2))
    half = 0.5 * (1.0 + t)
    slope = half + 0.5 * z * (1.0 - t * t) * (c * (1.0 + 3.0 * a * z2))
    return z * half, slope


def middle_kernel(nchunk, part, weight, gout, out, gh, gw,
                  opp_in, t_out, in_r, in_l, s_out, y_in, gl, send_sem, recv_sem, own_sem):
    blk, dev = col_place()
    wire = Wire(send_sem, recv_sem)
    rows = gout.shape[0] // nchunk
    to = {"R": dev(0, 1), "L": dev(0, -1), "Y": dev(1, 0)}
    barrier(list(to.values()))
    cut = lambda k: pl.ds(k * rows, rows)
    f = lambda v: v.astype(f32)
    chunks = range(nchunk)
    way_of = lambda k: "R" if k % 2 == 0 else "L"
    side = {"R": 1, "L": -1}
    arrive = {"R": in_r, "L": in_l}
    other = {"R": "L", "L": "R"}

    for k in chunks:
        for p in (1, 0):
            wire.push(("opp", p, k), part.at[blk(p, 2), cut(k)], opp_in.at[p, cut(k)], to[way_of(k)])
    for k in chunks:
        w = other[way_of(k)]
        for p in (1, 0):
            wire.push((w, p, k), part.at[blk(p, side[w]), cut(k)], arrive[w].at[p, cut(k)], to[w])

    def stage2(k):
        w = way_of(k)
        for p in (1, 0):
            wire.take(("opp", p, k), opp_in.at[p, cut(k)], to["Y"])
            t_out[p, cut(k)] = (f(part[blk(p, side[w]), cut(k)]) + f(opp_in[p, cut(k)])).astype(bf16)
            wire.push((w, p, k), t_out.at[p, cut(k)], arrive[w].at[p, cut(k)], to[w])

    def ring_sum(p, k):
        for w in "RL":
            wire.take((w, p, k), arrive[w].at[p, cut(k)], to["Y"])
        return f(part[blk(p, 0), cut(k)]) + f(in_r[p, cut(k)]) + f(in_l[p, cut(k)])

    def stage3(k):
        s_out[cut(k)] = ring_sum(1, k).astype(bf16)
        wire.push(("y", k), s_out.at[cut(k)], y_in.at[cut(k)], to["Y"])

    i0 = lax.broadcasted_iota(i32, (rows, rows), 0)
    i1 = lax.broadcasted_iota(i32, (rows, rows), 1)
    inside = i0 % BLOCK
    node = i0 - inside + jnp.where(inside < BLOCK // 2, 2 * inside, 2 * inside - (BLOCK - 1))
    order = (node == i1).astype(f32).astype(bf16)
    locals_ = []

    def stage4(k):
        total = ring_sum(0, k)
        wire.take(("y", k), y_in.at[cut(k)], to["Y"])
        hidden = (total + f(y_in[cut(k)])).astype(bf16)
        w = weight[...]
        pre = jnp.dot(hidden, w, preferred_element_type=f32)
        go = jnp.dot(order, gout[cut(k)], preferred_element_type=f32)
        act, slope = gelu_both(pre)
        gp = (go * slope).astype(bf16)
        gl[cut(k)] = lax.dot_general(gp, w, (((1,), (1,)), ((), ())), preferred_element_type=f32).astype(bf16)
        for way in "YRL":
            wire.push(("g" + way, 0, 0, k), gl.at[cut(k)], gh.at[blk(0, 0), cut(k)], to[way])
        own = pltpu.make_async_copy(gl.at[cut(k)], gh.at[blk(0, 0), cut(k)], own_sem.at[k])
        own.start()
        locals_.append(own)
        out[cut(k)] = lax.dot_general(order, act.astype(bf16), (((0,), (0,)), ((), ())),
                                      preferred_element_type=f32).astype(bf16)
        term = lax.dot_general(hidden, gp, (((0,), (0,)), ((), ())), preferred_element_type=f32)
        if k == 0:
            gw[...] = term
        else:
            gw[...] += term

    def stage5(k):
        spot = gh.at[blk(1, 0), cut(k)]
        wire.take(("gY", 0, 0, k), spot, to["Y"])
        for way in "RL":
            wire.push(("g" + way, 1, 0, k), spot, spot, to[way])

    def stage6(k):
        for p in (0, 1):
            for way in "RL":
                d = -side[way]
                spot = gh.at[blk(p, d), cut(k)]
                wire.take(("g" + way, p, 0, k), spot, to["Y"])
                if way == way_of(k):
                    wire.push(("g" + way, p, 1, k), spot, spot, to[way])

    def stage7(k):
        for p in (0, 1):
            wire.take(("g" + way_of(k), p, 1, k), gh.at[blk(p, 2), cut(k)], to["Y"])

    for k in chunks:
        stage2(k)
    stages = [stage3, stage4, stage5, stage6, stage7]
    for tick in range(nchunk + len(stages) - 1):
        for s, stage in enumerate(stages):
            if 0 <= tick - s < nchunk:
                stage(tick - s)
    for own in locals_:
        own.wait()
    wire.drain()


def middle(part, weight, gout, nchunk=4, cid=2):
    rows, width = gout.shape
    n = part.shape[0]
    piece = lambda *lead: pltpu.VMEM(lead + (rows, width), bf16)
    return pl.pallas_call(
        functools.partial(middle_kernel, nchunk),
        out_shape=[jax.ShapeDtypeStruct((rows, width), bf16),
                   jax.ShapeDtypeStruct((n, rows, width), bf16),
                   jax.ShapeDtypeStruct((width, width), f32)],
        in_specs=[pl.BlockSpec(memory_space=VM)] * 3,
        out_specs=[pl.BlockSpec(memory_space=VM), pl.BlockSpec(memory_space=ANY), pl.BlockSpec(memory_space=VM)],
        scratch_shapes=[piece(2), piece(2), piece(2), piece(2), piece(), piece(), piece(),
                        pltpu.SemaphoreType.DMA((128,)), pltpu.SemaphoreType.DMA((128,)),
                        pltpu.SemaphoreType.DMA((nchunk,))],
        compiler_params=pltpu.CompilerParams(collective_id=cid, has_side_effects=True, vmem_limit_bytes=48 << 20),
        name="middle",
    )(part, weight, gout)


def last_kernel(nchunk, part, term, out, gw,
                sib_in, opp_out, opp_in, d_out, t_out, in_r, in_l, s_out, y_in,
                w_sib, w_half, w_row, w_col, w_sum, w_full, send_sem, recv_sem):
    blk, dev, core = row_place()
    cblk, cdev = col_place()
    wire = Wire(send_sem, recv_sem)
    rows = out.shape[0] // nchunk
    to = {"R": dev(0, 1), "L": dev(0, -1), "Y": dev(1, 0), "S": dev(0, 0, 1)}
    peers = [(p, d) for p in (0, 1) for d in range(RING) if (p, d) != (0, 0)]
    barrier([to["S"]] + [dev(p, d) for p, d in peers] + [cdev(p, d) for p, d in peers])
    cut = lambda k: pl.ds(k * rows, rows)
    f = lambda v: v.astype(f32)
    chunks = range(nchunk)
    way_of = lambda k: "R" if k % 2 == 0 else "L"
    side = {"R": 1, "L": -1}
    arrive = {"R": in_r, "L": in_l}
    other = {"R": "L", "L": "R"}
    rel = lambda p, d: p * RING + d % RING

    half = term.shape[0] // 2
    ninth = half // (2 * RING)
    hd = lambda c: pl.ds(pl.multiple_of(c * half, half), half)
    seat = lambda p, d: blk(p, d) // 2
    sd = lambda j: pl.ds(pl.multiple_of(j * ninth, ninth), ninth)
    wire.push("w0", term.at[hd(1 - core)], w_sib, to["S"])

    def sib(p, d, k):
        wire.push(("s", rel(p, d), k), part.at[blk(p, d, 1), cut(k)], sib_in.at[rel(p, d), cut(k)], to["S"])

    for k in chunks:
        for p in (1, 0):
            sib(p, 2, k)
    for k in chunks:
        for p in (1, 0):
            sib(p, side[other[way_of(k)]], k)
    for k in chunks:
        for p in (1, 0):
            sib(p, side[way_of(k)], k)
    for k in chunks:
        for p in (1, 0):
            sib(p, 0, k)

    def both(p, d, k):
        wire.take(("s", rel(p, d), k), sib_in.at[rel(p, d), cut(k)], to["S"])
        return f(part[blk(p, d), cut(k)]) + f(sib_in[rel(p, d), cut(k)])

    for k in chunks:
        for p in (1, 0):
            opp_out[p, cut(k)] = both(p, 2, k).astype(bf16)
            wire.push(("opp", p, k), opp_out.at[p, cut(k)], opp_in.at[p, cut(k)], to[way_of(k)])
    for k in chunks:
        w = other[way_of(k)]
        for p in (1, 0):
            d_out[p, cut(k)] = both(p, side[w], k).astype(bf16)
            wire.push((w, p, k), d_out.at[p, cut(k)], arrive[w].at[p, cut(k)], to[w])

    wire.take("w0", w_sib, to["S"])
    w_half[...] = term[hd(core)] + w_sib[...]
    for i, (p, d) in enumerate(peers):
        wire.push(("w1", i), w_half.at[sd(seat(p, d))], w_row.at[i], dev(p, d))

    def stage2(k):
        w = way_of(k)
        for p in (1, 0):
            base = both(p, side[w], k)
            wire.take(("opp", p, k), opp_in.at[p, cut(k)], to["Y"])
            t_out[p, cut(k)] = (base + f(opp_in[p, cut(k)])).astype(bf16)
            wire.push((w, p, k), t_out.at[p, cut(k)], arrive[w].at[p, cut(k)], to[w])

    def ring_sum(p, k):
        base = both(p, 0, k)
        for w in "RL":
            wire.take((w, p, k), arrive[w].at[p, cut(k)], to["Y"])
        return base + f(in_r[p, cut(k)]) + f(in_l[p, cut(k)])

    def stage3(k):
        s_out[cut(k)] = ring_sum(1, k).astype(bf16)
        wire.push(("y", k), s_out.at[cut(k)], y_in.at[cut(k)], to["Y"])

    def stage4(k):
        total = ring_sum(0, k)
        wire.take(("y", k), y_in.at[cut(k)], to["Y"])
        out[cut(k)] = (total + f(y_in[cut(k)])).astype(bf16)

    for k in chunks:
        stage2(k)
        if k == 1:
            mine = w_half[sd(seat(0, 0))]
            for i, (p, d) in enumerate(peers):
                wire.take(("w1", i), w_row.at[i], to["Y"])
                mine = mine + w_row[i]
            w_sum[...] = mine
            here = cblk(0, 0)
            w_col[here] = mine
            for i, (p, d) in enumerate(peers):
                wire.push(("w2", i), w_sum, w_col.at[here], cdev(p, d))
    for i, (p, d) in enumerate(peers):
        wire.take(("w2", i), w_col.at[cblk(p, -d)], to["Y"])
    total = w_col[0]
    for i in range(1, 2 * RING):
        total = total + w_col[i]
    spot = lambda p, d: pl.ds(pl.multiple_of(core * half + seat(p, d) * ninth, ninth), ninth)
    w_full[spot(0, 0)] = total
    for i, (p, d) in enumerate(peers):
        wire.push(("w3", i), w_full.at[spot(0, 0)], w_full.at[spot(0, 0)], dev(p, d))
    stages = [stage3, stage4]
    for tick in range(nchunk + len(stages) - 1):
        for s, stage in enumerate(stages):
            if 0 <= tick - s < nchunk:
                stage(tick - s)
        if tick == 0:
            for i, (p, d) in enumerate(peers):
                wire.take(("w3", i), w_full.at[spot(p, -d)], to["Y"])
            wire.push("w4", w_full.at[hd(core)], w_full.at[hd(core)], to["S"])
    wire.take("w4", w_full.at[hd(1 - core)], to["S"])
    gw[...] = w_full[...]
    wire.drain()


def last(part, term, nchunk=4, cid=3):
    n, rows, width = part.shape
    piece = lambda *lead: pltpu.VMEM(lead + (rows, width), bf16)
    wrows = term.shape[0]
    wf = lambda *lead: pltpu.VMEM(lead + (term.shape[1],), f32)
    nine = wrows // (4 * RING)
    return pl.pallas_call(
        functools.partial(last_kernel, nchunk),
        out_shape=[jax.ShapeDtypeStruct((rows, width), bf16), jax.ShapeDtypeStruct(term.shape, f32)],
        in_specs=[pl.BlockSpec(memory_space=VM)] * 2,
        out_specs=[pl.BlockSpec(memory_space=VM)] * 2,
        scratch_shapes=[piece(n // 2), piece(2), piece(2), piece(2), piece(2), piece(2), piece(2), piece(), piece(),
                        wf(wrows // 2), wf(wrows // 2), wf(2 * RING - 1, nine), wf(2 * RING, nine), wf(nine), wf(wrows),
                        pltpu.SemaphoreType.DMA((160,)), pltpu.SemaphoreType.DMA((160,))],
        compiler_params=pltpu.CompilerParams(collective_id=cid, has_side_effects=True, vmem_limit_bytes=48 << 20),
        name="last",
    )(part, term)


def per_device(features, weight, grad_out, tile_rows, tile_cols, tile_values, tile_counts):
    nodes_dev, width = features.shape
    nr = nodes_dev * lax.axis_size("col") // BLOCK
    nc = nodes_dev * lax.axis_size("row") // BLOCK
    *lists, tot = make_meta(tile_rows, tile_cols, tile_counts, nr, nc)
    source, m = gather_rows(features, tile_values.reshape(tile_values.shape[2:]))
    part = spmm(fwd_kernel, lists[:3], tot, m, source.reshape(-1, width), nr, "spmm_fwd")
    output, grad_hidden, term = middle(part.reshape(-1, nodes_dev, width), weight, grad_out)
    back = spmm(bwd_kernel, lists[3:], tot, m, grad_hidden.reshape(-1, width), nc, "spmm_bwd")
    grad_feat, grad_weight = last(back.reshape(-1, nodes_dev, width), term)
    return output, grad_feat, grad_weight


def solution(mesh):
    placed = (
        P(("col", "row"), None),
        P(),
        P(("row", "col"), None),
        P("row", "col", None),
        P("row", "col", None),
        P("row", "col", None, None),
        P("row", "col"),
    )
    return jax.shard_map(
        per_device,
        mesh=mesh,
        in_specs=placed,
        out_specs=(P(("row", "col"), None), P(("col", "row"), None), P()),
        check_vma=False,
    )
```

```python
import functools

import jax
import jax.numpy as jnp
from jax import lax
from jax.experimental import pallas as pl
from jax.experimental.pallas import tpu as pltpu
from jax.sharding import PartitionSpec as P

BLOCK = 64
GROUP = 4
UNROLL = 16
RING = 4
LANES = 128
MESH = pl.DeviceIdType.MESH
VM = pltpu.VMEM
f32, bf16, i32 = jnp.float32, jnp.bfloat16, jnp.int32


def up(n, m):
    return -(-n // m) * m


def group_bound(tiles, blocks):
    return up((tiles + (GROUP - 1) * min(blocks, tiles)) // GROUP, UNROLL)


def lists_of(key_row, other_row, tiles, nb, groups_max, wide):
    tp = key_row.shape[1]
    nbp = up(nb, LANES)
    hot = (lax.broadcasted_iota(i32, (nbp, tp), 0) == key_row).astype(f32)
    hotb = hot.astype(bf16)
    count = jnp.sum(hot, axis=1, keepdims=True)
    upper = (lax.broadcasted_iota(i32, (tp, tp), 0) < lax.broadcasted_iota(i32, (tp, tp), 1)).astype(f32).astype(bf16)
    rank = jnp.dot(hotb, upper, preferred_element_type=f32)
    groups = jnp.floor((count + (GROUP - 1)) * (1.0 / GROUP))
    b0 = lax.broadcasted_iota(i32, (nbp, nbp), 0)
    b1 = lax.broadcasted_iota(i32, (nbp, nbp), 1)
    lower = (b1 < b0).astype(f32).astype(bf16)
    first = jnp.dot(lower, jnp.broadcast_to(groups, (nbp, LANES)).astype(bf16), preferred_element_type=f32)[:, :1]
    place = jnp.sum(hot * (rank + GROUP * first), axis=0, keepdims=True)
    live = jnp.sum(hot, axis=0, keepdims=True) > 0
    place = jnp.where(live, place, -1.0).astype(i32)
    spot = (lax.broadcasted_iota(i32, (wide, tp), 0) == place).astype(f32).astype(bf16)
    t = lax.broadcasted_iota(i32, (1, tp), 1)
    row = lax.broadcasted_iota(i32, (8, tp), 0)
    data = jnp.where(row == 0, t // 128, jnp.where(row == 1, t % 128, jnp.where(row == 2, other_row, 1)))
    got = lax.dot_general(data.astype(f32).astype(bf16), spot, (((1,), (1,)), ((), ())), preferred_element_type=f32)
    there = got[3:4] > 0
    tile = jnp.where(there, got[0:1] * 128 + got[1:2], float(tiles)).astype(i32)
    other = jnp.where(there, got[2:3], 0.0).astype(i32)
    g = lax.broadcasted_iota(i32, (nbp, wide), 1).astype(f32)
    starts = jnp.sum(jnp.where(jnp.logical_and(first == g, groups > 0), 1.0, 0.0), axis=0, keepdims=True).astype(i32)
    last = jnp.where(groups > 0, first + groups - 1, float(groups_max))
    last = jnp.sum(jnp.where(b0 == b1, last, 0.0), axis=0, keepdims=True).astype(i32)
    last = jnp.concatenate([last, jnp.zeros((1, wide - nbp), i32)], axis=1)
    return [tile, other, starts, last]


def lists_kernel(tiles, nr, nc, wide, rows_ref, cols_ref, count_ref, out_ref, keep):
    tp = keep.shape[1]
    keep[...] = jnp.zeros_like(keep)
    keep[0:1, :tiles] = rows_ref[...]
    keep[1:2, :tiles] = cols_ref[...]
    live = lax.broadcasted_iota(i32, (1, tp), 1) < count_ref[0, 0]
    rows, cols = keep[0:1], keep[1:2]
    fwd = lists_of(jnp.where(live, rows, 4096), cols, tiles, nr, group_bound(tiles, nr), wide)
    bwd = lists_of(jnp.where(live, cols, 4096), rows, tiles, nc, group_bound(tiles, nc), wide)
    for i, v in enumerate(fwd + bwd):
        out_ref[i:i + 1] = v


def make_lists(rows, cols, count, nr, nc):
    tiles = rows.shape[-1]
    wide = up(GROUP * max(group_bound(tiles, nr), group_bound(tiles, nc)), LANES)
    return pl.pallas_call(
        functools.partial(lists_kernel, tiles, nr, nc, wide),
        out_shape=jax.ShapeDtypeStruct((8, wide), i32),
        in_specs=[pl.BlockSpec(memory_space=VM)] * 2 + [pl.BlockSpec(memory_space=pltpu.SMEM)],
        out_specs=pl.BlockSpec(memory_space=VM),
        scratch_shapes=[pltpu.VMEM((8, up(tiles, LANES)), i32)],
        compiler_params=pltpu.CompilerParams(vmem_limit_bytes=48 << 20),
        name="lists",
    )(rows.reshape(1, tiles), cols.reshape(1, tiles), count)


class Wire:
    def __init__(self, send_sem, recv_sem):
        self.send_sem, self.recv_sem = send_sem, recv_sem
        self.ids, self.sent = {}, []

    def _sems(self, key):
        n = self.ids.setdefault(key, len(self.ids))
        assert n < self.send_sem.shape[0]
        return dict(send_sem=self.send_sem.at[n], recv_sem=self.recv_sem.at[n])

    def push(self, key, src, dst, dev):
        copy = pltpu.make_async_remote_copy(
            src_ref=src, dst_ref=dst, device_id=dev, device_id_type=MESH, **self._sems(key))
        copy.start()
        self.sent.append(copy)

    def take(self, key, dst, dev):
        pltpu.make_async_remote_copy(
            src_ref=dst, dst_ref=dst, device_id=dev, device_id_type=MESH, **self._sems(key)).wait_recv()

    def drain(self):
        for copy in self.sent:
            copy.wait_send()


def barrier(devs):
    sem = pltpu.get_barrier_semaphore()
    for dev in devs:
        pl.semaphore_signal(sem, inc=1, device_id=dev, device_id_type=MESH)
    pl.semaphore_wait(sem, len(devs))


def row_place():
    r = lax.axis_index("row")
    pair, ring, core = r // (2 * RING), (r // 2) % RING, r % 2

    def blk(p, d, s=0):
        return (pair + p) % 2 * (2 * RING) + (ring + d) % RING * 2 + (core + s) % 2

    return blk, (lambda p, d, s=0: {"row": blk(p, d, s)}), core


def col_place():
    c = lax.axis_index("col")
    pair, ring = c // RING, c % RING

    def blk(p, d):
        return (pair + p) % 2 * RING + (ring + d) % RING

    return blk, (lambda p, d: {"col": blk(p, d)})


def gelu_both(z):
    c, a = 0.7978845608, 0.044715
    z2 = z * z
    t = jnp.tanh(c * (z + a * z * z2))
    half = 0.5 * (1.0 + t)
    slope = half + 0.5 * z * (1.0 - t * t) * (c * (1.0 + 3.0 * a * z2))
    return z * half, slope


def swap_halves(m):
    return jnp.concatenate([m[:, BLOCK:], m[:, :BLOCK]], axis=1)


def weave(work, steps):
    done = 0
    for i, piece in enumerate(work):
        piece()
        goal = len(steps) * (i + 1) // len(work)
        while done < goal:
            steps[done]()
            done += 1


def step_of(fn, *args):
    return lambda: fn(*args)


def layer_kernel(lists, feat, values, weight, gout, out, gfeat, gw,
                 vals, m, src_0, src_1, runs, part,
                 c_opp, c_t, c_r, c_l, c_s, c_y, hid, gl, gh_0, gh_1, back,
                 sib_in, o_out, o_in, d_out, t_out, in_r, in_l, s_out, y_in,
                 term, w_sib, w_half, w_row, w_col, w_sum, w_full,
                 send_sem, recv_sem, val_sem):
    rblk, rdev, core = row_place()
    cblk, cdev = col_place()
    wire = Wire(send_sem, recv_sem)
    peers = [(p, d) for p in (0, 1) for d in range(RING) if (p, d) != (0, 0)]
    load = pltpu.make_async_copy(values, vals, val_sem)
    load.start()
    barrier([rdev(0, 0, 1)] + [rdev(p, d) for p, d in peers] + [cdev(p, d) for p, d in peers])

    f = lambda v: v.astype(f32)
    src, gh = (src_0, src_1), (gh_0, gh_1)
    tiles = vals.shape[0]
    nbd = feat.shape[0] // BLOCK
    nr, nc = part.shape[1], src_0.shape[0]
    gf, gb = group_bound(tiles, nr), group_bound(tiles, nc)
    row_to = {"R": rdev(0, 1), "L": rdev(0, -1), "Y": rdev(1, 0), "S": rdev(0, 0, 1)}
    col_to = {"R": cdev(0, 1), "L": cdev(0, -1), "Y": cdev(1, 0)}
    any_dev = row_to["S"]
    side = {"R": 1, "L": -1}
    other = {"R": "L", "L": "R"}

    cb = nbd // 2

    def gather(h):
        def slot(p, d, s, k, part_):
            size = cb if part_ is None else cb // 2
            at = rblk(p, d, s) * nbd + k * cb + (0 if part_ is None else part_ * size)
            return src[h].at[pl.ds(at, size)]

        def push(way, p, d, k, part_=None):
            spot = slot(p, d, 0, k, part_)
            wire.push(("f", h, way, p, d % RING, k, part_), spot, spot, row_to[way])

        def take(way, p, d, k, part_=None):
            key = ("f", h, way, p, d % RING, k, part_)
            if way == "S":
                wire.take(key, slot(p, d, 1, k, part_), any_dev)
                return
            q, e = {"R": (p, d - 1), "L": (p, d + 1), "Y": (1 - p, d)}[way]
            wire.take(key, slot(q, e, 0, k, part_), any_dev)
            if way == "Y":
                if k == 1:
                    push("R", q, e, k)
                    push("L", q, e, k)
            else:
                if abs(e) == 1:
                    push(way, q, e, k, 0 if way == "R" else 1)
                if k == 0:
                    push("Y", q, e, k, part_)
            push("S", q, e, k, part_)

        def own():
            here = pl.ds(rblk(0, 0) * nbd, nbd)
            src[h][here] = feat[:, h * LANES:(h + 1) * LANES].reshape(nbd, BLOCK, LANES)
            for k in (1, 0):
                for way in "YRL":
                    push(way, 0, 0, k)
            for k in (1, 0):
                push("S", 0, 0, k)

        order = [("Y", 0, 0, 1), ("R", 0, 0, 0), ("L", 0, 0, 0), ("Y", 0, 0, 0), ("R", 0, 0, 1), ("L", 0, 0, 1),
                 ("R", 0, -1, 0, 0), ("L", 0, 1, 0, 1), ("R", 1, 0, 1), ("L", 1, 0, 1),
                 ("Y", 0, -1, 0), ("Y", 0, 1, 0)]
        order += [("R", p, -1, 1, 0) if way == "R" else ("L", p, 1, 1, 1) for p in (0, 1) for way in "RL"]
        order += [("Y", 0, -2, 0, 0), ("Y", 0, 2, 0, 1)]
        steps = [step_of(take, *o) for o in order]

        def close():
            for key in [key for key in wire.ids if key[:3] == ("f", h, "S")]:
                take("S", *key[3:])

        return own, steps + [close]

    low = lax.broadcasted_iota(i32, (BLOCK // 2, 2 * BLOCK), 1) < BLOCK

    def lhs_fwd(g):
        v = [m[lists[0, g * GROUP + k]] for k in range(GROUP)]
        s = [swap_halves(x) for x in v]
        even = [jnp.where(low, v[0], s[1]), jnp.where(low, v[2], s[3])]
        odd = [jnp.where(low, s[0], v[1]), jnp.where(low, s[2], v[3])]
        return jnp.concatenate([jnp.concatenate(even, axis=1), jnp.concatenate(odd, axis=1)], axis=0)

    def rhs_fwd(h, g):
        return jnp.concatenate([src[h][lists[1, g * GROUP + k]] for k in range(GROUP)], axis=0)

    def lhs_bwd(g):
        w = jnp.concatenate([m[lists[4, g * GROUP + k]] for k in range(GROUP)], axis=0).T
        return jnp.concatenate([w[:BLOCK], w[BLOCK:]], axis=1)

    def rhs_bwd(h, g):
        v = [gh[h][lists[5, g * GROUP + k]] for k in range(GROUP)]
        return jnp.concatenate([x[:BLOCK // 2] for x in v] + [x[BLOCK // 2:] for x in v], axis=0)

    def products(h, lhs, rhs, flags, groups, pieces):
        state = [jnp.zeros((BLOCK, LANES), f32)]
        turns = groups // UNROLL

        def body(i, run):
            prods = []
            for u in range(UNROLL):
                g = i * UNROLL + u
                prods.append((g, jnp.dot(lhs(g), rhs(h, g), preferred_element_type=f32)))
            for g, p in prods:
                run = jnp.where(lists[flags, g] > 0, p, run + p)
                runs[g] = run.astype(bf16)
            return run

        def piece(i):
            lo, hi = turns * i // pieces, turns * (i + 1) // pieces
            state[0] = lax.fori_loop(lo, hi, body, state[0])

        return [step_of(piece, i) for i in range(pieces)]

    def settle(dst, h, lasts, groups, blocks):
        runs[groups] = jnp.zeros((BLOCK, LANES), bf16)

        def body(i, _):
            for u in range(8):
                dst[h, i * 8 + u] = runs[lists[lasts, i * 8 + u]]
            return 0

        lax.fori_loop(0, blocks // 8, body, 0)

    nk = 4
    ck = nbd // nk
    chunks = range(nk)
    way_of = lambda k: "R" if k % 2 == 0 else "L"
    cut = lambda k: pl.ds(k * ck, ck)
    blk_cut = lambda b, k: pl.ds(b * nbd + k * ck, ck)
    c_in = {"R": c_r, "L": c_l}

    def c_start(h):
        for k in chunks:
            for p in (1, 0):
                wire.push(("c", h, "opp", p, k), part.at[h, blk_cut(cblk(p, 2), k)], c_opp.at[h, p, cut(k)], col_to[way_of(k)])
        for k in chunks:
            w = other[way_of(k)]
            for p in (1, 0):
                wire.push(("c", h, w, p, k), part.at[h, blk_cut(cblk(p, side[w]), k)], c_in[w].at[h, p, cut(k)], col_to[w])

    def c_ring(h, k):
        w = way_of(k)
        for p in (1, 0):
            wire.take(("c", h, "opp", p, k), c_opp.at[h, p, cut(k)], any_dev)
            c_t[h, p, cut(k)] = (f(part[h, blk_cut(cblk(p, side[w]), k)]) + f(c_opp[h, p, cut(k)])).astype(bf16)
            wire.push(("c", h, w, p, k), c_t.at[h, p, cut(k)], c_in[w].at[h, p, cut(k)], col_to[w])

    def c_sum(h, p, k):
        for w in "RL":
            wire.take(("c", h, w, p, k), c_in[w].at[h, p, cut(k)], any_dev)
        return f(part[h, blk_cut(cblk(p, 0), k)]) + f(c_r[h, p, cut(k)]) + f(c_l[h, p, cut(k)])

    def c_pair(h, k):
        c_s[h, cut(k)] = c_sum(h, 1, k).astype(bf16)
        wire.push(("c", h, "y", k), c_s.at[h, cut(k)], c_y.at[h, cut(k)], col_to["Y"])

    def c_end(h, k):
        total = c_sum(h, 0, k)
        wire.take(("c", h, "y", k), c_y.at[h, cut(k)], any_dev)
        hid[h, cut(k)] = (total + f(c_y[h, cut(k)])).astype(bf16)

    rows = ck * BLOCK
    i0 = lax.broadcasted_iota(i32, (rows, rows), 0)
    i1 = lax.broadcasted_iota(i32, (rows, rows), 1)
    inside = i0 % BLOCK
    node = i0 - inside + jnp.where(inside < BLOCK // 2, 2 * inside, 2 * inside - (BLOCK - 1))
    order = (node == i1).astype(f32).astype(bf16)

    def g_push(h, k):
        for way in "YRL":
            wire.push(("g", h, way, 0, 0, k), gl.at[h, cut(k)], gh[h].at[blk_cut(cblk(0, 0), k)], col_to[way])

    def dense(k):
        hidden = jnp.concatenate([hid[h, cut(k)].reshape(rows, LANES) for h in (0, 1)], axis=1)
        w = weight[...]
        at = pl.ds(k * rows, rows)
        pre = jnp.dot(hidden, w, preferred_element_type=f32)
        go = jnp.dot(order, gout[at], preferred_element_type=f32)
        act, slope = gelu_both(pre)
        gp = (go * slope).astype(bf16)
        local = lax.dot_general(gp, w, (((1,), (1,)), ((), ())), preferred_element_type=f32).astype(bf16)
        for h in (0, 1):
            mine = local[:, h * LANES:(h + 1) * LANES].reshape(ck, BLOCK, LANES)
            gl[h, cut(k)] = mine
        g_push(0, k)
        for h in (0, 1):
            gh[h][blk_cut(cblk(0, 0), k)] = gl[h, cut(k)]
        out[at] = lax.dot_general(order, act.astype(bf16), (((0,), (0,)), ((), ())),
                                  preferred_element_type=f32).astype(bf16)
        t = lax.dot_general(hidden, gp, (((0,), (0,)), ((), ())), preferred_element_type=f32)
        if k == 0:
            term[...] = t
        else:
            term[...] += t

    def g_pair(h, k):
        spot = gh[h].at[blk_cut(cblk(1, 0), k)]
        wire.take(("g", h, "Y", 0, 0, k), spot, any_dev)
        for way in "RL":
            wire.push(("g", h, way, 1, 0, k), spot, spot, col_to[way])

    def g_ring(h, k):
        for p in (0, 1):
            for way in "RL":
                spot = gh[h].at[blk_cut(cblk(p, -side[way]), k)]
                wire.take(("g", h, way, p, 0, k), spot, any_dev)
                if way == way_of(k):
                    wire.push(("g", h, way, p, 1, k), spot, spot, col_to[way])

    def g_far(h, k):
        for p in (0, 1):
            wire.take(("g", h, way_of(k), p, 1, k), gh[h].at[blk_cut(cblk(p, 2), k)], any_dev)

    r_in = {"R": in_r, "L": in_l}
    rel = lambda p, d: p * RING + d % RING
    arrived = set()

    def r_start(h):
        for d in (2, 1, -1, 0):
            for p in (1, 0):
                there = pl.ds(rblk(p, d, 1) * nbd, nbd)
                wire.push(("s", h, rel(p, d)), back.at[h, there], sib_in.at[h, rel(p, d)], row_to["S"])

    def both(h, p, d, k):
        key = ("s", h, rel(p, d))
        if key not in arrived:
            arrived.add(key)
            wire.take(key, sib_in.at[h, rel(p, d)], any_dev)
        return f(back[h, blk_cut(rblk(p, d), k)]) + f(sib_in[h, rel(p, d), cut(k)])

    def r_far(h, k):
        for p in (1, 0):
            o_out[h, p, cut(k)] = both(h, p, 2, k).astype(bf16)
            wire.push(("r", h, "opp", p, k), o_out.at[h, p, cut(k)], o_in.at[h, p, cut(k)], row_to[way_of(k)])

    def r_near(h, k):
        w = other[way_of(k)]
        for p in (1, 0):
            d_out[h, p, cut(k)] = both(h, p, side[w], k).astype(bf16)
            wire.push(("r", h, w, p, k), d_out.at[h, p, cut(k)], r_in[w].at[h, p, cut(k)], row_to[w])

    def r_ring(h, k):
        w = way_of(k)
        for p in (1, 0):
            base = both(h, p, side[w], k)
            wire.take(("r", h, "opp", p, k), o_in.at[h, p, cut(k)], any_dev)
            t_out[h, p, cut(k)] = (base + f(o_in[h, p, cut(k)])).astype(bf16)
            wire.push(("r", h, w, p, k), t_out.at[h, p, cut(k)], r_in[w].at[h, p, cut(k)], row_to[w])

    def r_sum(h, p, k):
        base = both(h, p, 0, k)
        for w in "RL":
            wire.take(("r", h, w, p, k), r_in[w].at[h, p, cut(k)], any_dev)
        return base + f(in_r[h, p, cut(k)]) + f(in_l[h, p, cut(k)])

    def r_pair(h, k):
        s_out[h, cut(k)] = r_sum(h, 1, k).astype(bf16)
        wire.push(("r", h, "y", k), s_out.at[h, cut(k)], y_in.at[h, cut(k)], row_to["Y"])

    def r_end(h, k):
        total = r_sum(h, 0, k)
        wire.take(("r", h, "y", k), y_in.at[h, cut(k)], any_dev)
        total = (total + f(y_in[h, cut(k)])).astype(bf16)
        gfeat[pl.ds(k * rows, rows), h * LANES:(h + 1) * LANES] = total.reshape(rows, LANES)

    def pipeline(stages, n):
        return [step_of(stage, k) for tick in range(n + len(stages) - 1)
                for s, stage in enumerate(stages) for k in [tick - s] if 0 <= k < n]

    def r_steps(h):
        steps = [step_of(r_far, h, k) for k in chunks] + [step_of(r_near, h, k) for k in chunks]
        steps += [step_of(r_ring, h, k) for k in chunks]
        return steps + pipeline([lambda k: r_pair(h, k), lambda k: r_end(h, k)], nk)

    half = term.shape[0] // 2
    eighth = half // (2 * RING)
    hd = lambda c: pl.ds(pl.multiple_of(c * half, half), half)
    seat = lambda p, d: rblk(p, d) // 2
    sd = lambda j: pl.ds(pl.multiple_of(j * eighth, eighth), eighth)
    spot_of = lambda p, d: pl.ds(pl.multiple_of(core * half + seat(p, d) * eighth, eighth), eighth)

    def w0():
        wire.push("w0", term.at[hd(1 - core)], w_sib, row_to["S"])

    def w1():
        wire.take("w0", w_sib, any_dev)
        w_half[...] = term[hd(core)] + w_sib[...]
        for i, (p, d) in enumerate(peers):
            wire.push(("w1", i), w_half.at[sd(seat(p, d))], w_row.at[i], rdev(p, d))

    def w2():
        mine = w_half[sd(seat(0, 0))]
        for i, _ in enumerate(peers):
            wire.take(("w1", i), w_row.at[i], any_dev)
            mine = mine + w_row[i]
        w_sum[...] = mine
        here = cblk(0, 0)
        w_col[here] = mine
        for i, (p, d) in enumerate(peers):
            wire.push(("w2", i), w_sum, w_col.at[here], cdev(p, d))

    def w3():
        for i, (p, d) in enumerate(peers):
            wire.take(("w2", i), w_col.at[cblk(p, -d)], any_dev)
        total = w_col[0]
        for i in range(1, 2 * RING):
            total = total + w_col[i]
        w_full[spot_of(0, 0)] = total
        for i, (p, d) in enumerate(peers):
            wire.push(("w3", i), w_full.at[spot_of(0, 0)], w_full.at[spot_of(0, 0)], rdev(p, d))

    def w4():
        for i, (p, d) in enumerate(peers):
            wire.take(("w3", i), w_full.at[spot_of(p, -d)], any_dev)
        wire.push("w4", w_full.at[hd(core)], w_full.at[hd(core)], row_to["S"])

    def w5():
        wire.take("w4", w_full.at[hd(1 - core)], any_dev)
        gw[...] = w_full[...]

    own0, steps0 = gather(0)
    own1, steps1 = gather(1)
    own0()
    load.wait()
    for s in range(0, tiles, 16):
        m[s:s + 16] = vals[s:s + 16].reshape((16,) + m.shape[1:])
    m[tiles:] = jnp.zeros((1,) + m.shape[1:], bf16)
    for i, step in enumerate(steps0):
        step()
        if i == 5:
            own1()
    weave(products(0, lhs_fwd, rhs_fwd, 2, gf, 7), steps1[:-1])
    settle(part, 0, 3, gf, nr)
    c_start(0)
    steps1[-1]()
    c_steps = [step_of(c_ring, 0, k) for k in chunks]
    c_steps += pipeline([lambda k: c_pair(0, k), lambda k: c_end(0, k)], nk)
    weave(products(1, lhs_fwd, rhs_fwd, 2, gf, 7), c_steps)
    settle(part, 1, 3, gf, nr)
    c_start(1)
    for k in chunks:
        c_ring(1, k)
    def finish(k):
        c_end(1, k)
        dense(k)

    for step in pipeline([lambda k: c_pair(1, k), finish, lambda k: g_pair(0, k)], nk):
        step()
    for k in chunks:
        g_push(1, k)
    w0()
    for step in pipeline([lambda k: g_ring(0, k), lambda k: g_far(0, k)], nk):
        step()
    g_steps = [step_of(g_pair, 1, k) for k in chunks] + [w1] + [step_of(g_ring, 1, k) for k in chunks] + [w2]
    g_steps += [step_of(g_far, 1, k) for k in chunks] + [w3]
    weave(products(0, lhs_bwd, rhs_bwd, 6, gb, 9), g_steps)
    settle(back, 0, 7, gb, nc)
    r_start(0)
    weave(products(1, lhs_bwd, rhs_bwd, 6, gb, 9), r_steps(0) + [w4])
    settle(back, 1, 7, gb, nc)
    r_start(1)
    for step in r_steps(1):
        step()
    w5()
    wire.drain()


def layer(lists, features, values, weight, grad_out, nr, nc):
    rows, width = features.shape
    tiles = values.shape[0]
    nbd = rows // BLOCK
    gmax = max(group_bound(tiles, nr), group_bound(tiles, nc))
    wrows = weight.shape[0]
    piece = lambda *lead: pltpu.VMEM(lead + (BLOCK, LANES), bf16)
    wf = lambda *lead: pltpu.VMEM(lead + (wrows,), f32)
    eighth = wrows // (4 * RING)
    two = 2
    scratch = [
        pltpu.VMEM(values.shape, bf16), pltpu.VMEM((tiles + 1, BLOCK // 2, 2 * BLOCK), bf16),
        piece(nc), piece(nc), piece(gmax + 1), piece(two, nr),
        piece(two, 2, nbd), piece(two, 2, nbd), piece(two, 2, nbd), piece(two, 2, nbd),
        piece(two, nbd), piece(two, nbd), piece(two, nbd), piece(two, nbd), piece(nr), piece(nr), piece(two, nc),
        piece(two, 2 * RING, nbd), piece(two, 2, nbd), piece(two, 2, nbd), piece(two, 2, nbd), piece(two, 2, nbd),
        piece(two, 2, nbd), piece(two, 2, nbd), piece(two, nbd), piece(two, nbd),
        wf(wrows), wf(wrows // 2), wf(wrows // 2), wf(2 * RING - 1, eighth), wf(2 * RING, eighth), wf(eighth), wf(wrows),
        pltpu.SemaphoreType.DMA((400,)), pltpu.SemaphoreType.DMA((400,)), pltpu.SemaphoreType.DMA,
    ]
    return pl.pallas_call(
        layer_kernel,
        out_shape=[jax.ShapeDtypeStruct((rows, width), bf16), jax.ShapeDtypeStruct((rows, width), bf16),
                   jax.ShapeDtypeStruct((wrows, width), f32)],
        in_specs=[pl.BlockSpec(memory_space=pltpu.SMEM), pl.BlockSpec(memory_space=VM), pl.BlockSpec(memory_space=pl.ANY),
                  pl.BlockSpec(memory_space=VM), pl.BlockSpec(memory_space=VM)],
        out_specs=[pl.BlockSpec(memory_space=VM)] * 3,
        scratch_shapes=scratch,
        compiler_params=pltpu.CompilerParams(collective_id=1, has_side_effects=True, vmem_limit_bytes=60 << 20),
        name="layer",
    )(lists, features, values, weight, grad_out)


def per_device(features, weight, grad_out, tile_rows, tile_cols, tile_values, tile_counts):
    nodes_dev = features.shape[0]
    nr = nodes_dev * lax.axis_size("col") // BLOCK
    nc = nodes_dev * lax.axis_size("row") // BLOCK
    lists = make_lists(tile_rows, tile_cols, tile_counts, nr, nc)
    values = tile_values.reshape(tile_values.shape[2:])
    return tuple(layer(lists, features, values, weight, grad_out, nr, nc))


def solution(mesh):
    placed = (
        P(("col", "row"), None),
        P(),
        P(("row", "col"), None),
        P("row", "col", None),
        P("row", "col", None),
        P("row", "col", None, None),
        P("row", "col"),
    )
    return jax.shard_map(
        per_device,
        mesh=mesh,
        in_specs=placed,
        out_specs=(P(("row", "col"), None), P(("col", "row"), None), P()),
        check_vma=False,
    )
```

```python
import functools

import jax
import jax.numpy as jnp
from jax import lax
from jax.experimental import pallas as pl
from jax.experimental.pallas import tpu as pltpu
from jax.sharding import PartitionSpec as P

BLOCK = 64
GROUP = 4
UNROLL = 16
RING = 4
LANES = 128
MESH = pl.DeviceIdType.MESH
VM = pltpu.VMEM
f32, bf16, i32 = jnp.float32, jnp.bfloat16, jnp.int32


def up(n, m):
    return -(-n // m) * m


def group_bound(tiles, blocks):
    return up((tiles + (GROUP - 1) * min(blocks, tiles)) // GROUP, UNROLL)


def lists_of(key_row, other_row, tiles, nb, groups_max, wide):
    tp = key_row.shape[1]
    nbp = up(nb, LANES)
    hot = (lax.broadcasted_iota(i32, (nbp, tp), 0) == key_row).astype(f32)
    hotb = hot.astype(bf16)
    count = jnp.sum(hot, axis=1, keepdims=True)
    upper = (lax.broadcasted_iota(i32, (tp, tp), 0) < lax.broadcasted_iota(i32, (tp, tp), 1)).astype(f32).astype(bf16)
    rank = jnp.dot(hotb, upper, preferred_element_type=f32)
    groups = jnp.floor((count + (GROUP - 1)) * (1.0 / GROUP))
    b0 = lax.broadcasted_iota(i32, (nbp, nbp), 0)
    b1 = lax.broadcasted_iota(i32, (nbp, nbp), 1)
    lower = (b1 < b0).astype(f32).astype(bf16)
    first = jnp.dot(lower, jnp.broadcast_to(groups, (nbp, LANES)).astype(bf16), preferred_element_type=f32)[:, :1]
    place = jnp.sum(hot * (rank + GROUP * first), axis=0, keepdims=True)
    live = jnp.sum(hot, axis=0, keepdims=True) > 0
    place = jnp.where(live, place, -1.0).astype(i32)
    spot = (lax.broadcasted_iota(i32, (wide, tp), 0) == place).astype(f32).astype(bf16)
    t = lax.broadcasted_iota(i32, (1, tp), 1)
    row = lax.broadcasted_iota(i32, (8, tp), 0)
    data = jnp.where(row == 0, t // 128, jnp.where(row == 1, t % 128, jnp.where(row == 2, other_row, 1)))
    got = lax.dot_general(data.astype(f32).astype(bf16), spot, (((1,), (1,)), ((), ())), preferred_element_type=f32)
    there = got[3:4] > 0
    tile = jnp.where(there, got[0:1] * 128 + got[1:2], float(tiles)).astype(i32)
    other = jnp.where(there, got[2:3], 0.0).astype(i32)
    g = lax.broadcasted_iota(i32, (nbp, wide), 1).astype(f32)
    starts = jnp.sum(jnp.where(jnp.logical_and(first == g, groups > 0), 1.0, 0.0), axis=0, keepdims=True).astype(i32)
    last = jnp.where(groups > 0, first + groups - 1, float(groups_max))
    last = jnp.sum(jnp.where(b0 == b1, last, 0.0), axis=0, keepdims=True).astype(i32)
    last = jnp.concatenate([last, jnp.zeros((1, wide - nbp), i32)], axis=1)
    return [tile, other, starts, last]


def lists_kernel(tiles, nr, nc, rows_in, cols_in, count_ref, out_ref, t_rows, t_cols, keep, sems):
    loads = [pltpu.make_async_copy(rows_in, t_rows, sems.at[0]), pltpu.make_async_copy(cols_in, t_cols, sems.at[1])]
    for load in loads:
        load.start()
    keep[...] = jnp.zeros_like(keep)
    for load in loads:
        load.wait()
    wide = out_ref.shape[1]
    keep[0:1, :tiles] = t_rows[0]
    keep[1:2, :tiles] = t_cols[0]
    rows, cols = keep[0:1], keep[1:2]
    live = lax.broadcasted_iota(i32, rows.shape, 1) < count_ref[0, 0]
    fwd = lists_of(jnp.where(live, rows, 4096), cols, tiles, nr, group_bound(tiles, nr), wide)
    bwd = lists_of(jnp.where(live, cols, 4096), rows, tiles, nc, group_bound(tiles, nc), wide)
    for i, v in enumerate(fwd + bwd):
        out_ref[i:i + 1] = v


def make_lists(rows, cols, count, nr, nc):
    tiles = rows.shape[-1]
    wide = up(GROUP * max(group_bound(tiles, nr), group_bound(tiles, nc)), LANES)
    return pl.pallas_call(
        functools.partial(lists_kernel, tiles, nr, nc),
        out_shape=jax.ShapeDtypeStruct((8, wide), i32),
        in_specs=[pl.BlockSpec(memory_space=pl.ANY)] * 2 + [pl.BlockSpec(memory_space=pltpu.SMEM)],
        out_specs=pl.BlockSpec(memory_space=VM),
        scratch_shapes=[pltpu.VMEM(rows.shape, i32), pltpu.VMEM(cols.shape, i32), pltpu.VMEM((8, up(tiles, LANES)), i32),
                        pltpu.SemaphoreType.DMA((2,))],
        compiler_params=pltpu.CompilerParams(vmem_limit_bytes=60 << 20),
        name="lists",
    )(rows, cols, count)


class Wire:
    def __init__(self, send_sem, recv_sem):
        self.send_sem, self.recv_sem = send_sem, recv_sem
        self.ids, self.sent = {}, []

    def _sems(self, key):
        n = self.ids.setdefault(key, len(self.ids))
        assert n < self.send_sem.shape[0]
        return dict(send_sem=self.send_sem.at[n], recv_sem=self.recv_sem.at[n])

    def push(self, key, src, dst, dev):
        copy = pltpu.make_async_remote_copy(
            src_ref=src, dst_ref=dst, device_id=dev, device_id_type=MESH, **self._sems(key))
        copy.start()
        self.sent.append(copy)

    def take(self, key, dst, dev):
        pltpu.make_async_remote_copy(
            src_ref=dst, dst_ref=dst, device_id=dev, device_id_type=MESH, **self._sems(key)).wait_recv()

    def drain(self):
        for copy in self.sent:
            copy.wait_send()


def greet(devs):
    sem = pltpu.get_barrier_semaphore()
    for dev in devs:
        pl.semaphore_signal(sem, inc=1, device_id=dev, device_id_type=MESH)
    return lambda: pl.semaphore_wait(sem, len(devs))


def row_place():
    r = lax.axis_index("row")
    pair, ring, core = r // (2 * RING), (r // 2) % RING, r % 2

    def blk(p, d, s=0):
        return (pair + p) % 2 * (2 * RING) + (ring + d) % RING * 2 + (core + s) % 2

    return blk, (lambda p, d, s=0: {"row": blk(p, d, s)}), core


def col_place():
    c = lax.axis_index("col")
    pair, ring = c // RING, c % RING

    def blk(p, d):
        return (pair + p) % 2 * RING + (ring + d) % RING

    return blk, (lambda p, d: {"col": blk(p, d)})


def gelu_both(z):
    c, a = 0.7978845608, 0.044715
    z2 = z * z
    t = jnp.tanh(c * (z + a * z * z2))
    half = 0.5 * (1.0 + t)
    slope = half + 0.5 * z * (1.0 - t * t) * (c * (1.0 + 3.0 * a * z2))
    return z * half, slope


def swap_halves(m):
    return jnp.concatenate([m[:, BLOCK:], m[:, :BLOCK]], axis=1)


def step_of(fn, *args):
    return lambda: fn(*args)


def layer_kernel(lists, feat_in, weight_in, gout_in, values_in, out, gfeat, gw,
                 feat, weight, gout, vals, m, src_0, src_1, runs, part,
                 c_bufs, hid, gl, gh_0, gh_1, back, sib_in, r_bufs,
                 term, w_sib, w_half, w_row, w_col, w_sum, w_full,
                 send_sem, recv_sem, load_sem):
    rblk, rdev, core = row_place()
    cblk, cdev = col_place()
    wire = Wire(send_sem, recv_sem)
    peers = [(p, d) for p in (0, 1) for d in range(RING) if (p, d) != (0, 0)]
    met = greet([rdev(0, 0, 1)] + [rdev(p, d) for p, d in peers] + [cdev(p, d) for p, d in peers])
    loads = [pltpu.make_async_copy(a, b, load_sem.at[i]) for i, (a, b) in enumerate([
        (feat_in, feat), (values_in, vals), (weight_in, weight), (gout_in, gout)])]
    for load in loads:
        load.start()

    f = lambda v: v.astype(f32)
    src, gh = (src_0, src_1), (gh_0, gh_1)
    tiles = vals.shape[0]
    nbd = feat.shape[0] // BLOCK
    nr, nc = part.shape[1], src_0.shape[0]
    gf, gb = group_bound(tiles, nr), group_bound(tiles, nc)
    row_to = {"R": rdev(0, 1), "L": rdev(0, -1), "Y": rdev(1, 0), "S": rdev(0, 0, 1)}
    col_to = {"R": cdev(0, 1), "L": cdev(0, -1), "Y": cdev(1, 0)}
    any_dev = row_to["S"]
    side = {"R": 1, "L": -1}
    other = {"R": "L", "L": "R"}

    cb = nbd // 2

    def gather(h):
        def slot(p, d, s, k, part_):
            size = cb if part_ is None else cb // 2
            at = rblk(p, d, s) * nbd + k * cb + (0 if part_ is None else part_ * size)
            return src[h].at[pl.ds(at, size)]

        def push(way, p, d, k, part_=None):
            spot = slot(p, d, 0, k, part_)
            wire.push(("f", h, way, p, d % RING, k, part_), spot, spot, row_to[way])

        def take(way, p, d, k, part_=None):
            key = ("f", h, way, p, d % RING, k, part_)
            if way == "S":
                wire.take(key, slot(p, d, 1, k, part_), any_dev)
                return
            q, e = {"R": (p, d - 1), "L": (p, d + 1), "Y": (1 - p, d)}[way]
            wire.take(key, slot(q, e, 0, k, part_), any_dev)
            if way == "Y":
                if k == 1:
                    push("R", q, e, k)
                    push("L", q, e, k)
            else:
                if abs(e) == 1:
                    push(way, q, e, k, 0 if way == "R" else 1)
                if k == 0:
                    push("Y", q, e, k, part_)
            push("S", q, e, k, part_)

        def own():
            push("Y", 0, 0, 1)
            for k in (0, 1):
                for way in "RL":
                    push(way, 0, 0, k)
            for k in (0, 1):
                push("S", 0, 0, k)

        def own_late():
            push("Y", 0, 0, 0)

        order = [("Y", 0, 0, 1), ("R", 0, 0, 0), ("L", 0, 0, 0), ("R", 0, 0, 1), ("L", 0, 0, 1),
                 ("R", 0, -1, 0, 0), ("L", 0, 1, 0, 1), ("R", 1, 0, 1), ("L", 1, 0, 1),
                 ("Y", 0, 0, 0), ("Y", 0, -1, 0), ("Y", 0, 1, 0)]
        order += [("R", p, -1, 1, 0) if way == "R" else ("L", p, 1, 1, 1) for p in (0, 1) for way in "RL"]
        order += [("Y", 0, -2, 0, 0), ("Y", 0, 2, 0, 1)]
        steps = [step_of(take, *o) for o in order]
        first = steps[2]

        def third():
            first()
            own_late()

        steps[2] = third

        def close():
            for key in [key for key in wire.ids if key[:3] == ("f", h, "S")]:
                take("S", *key[3:])

        return own, steps + [close]

    low = lax.broadcasted_iota(i32, (BLOCK // 2, 2 * BLOCK), 1) < BLOCK

    def lhs_fwd(g):
        v = [m[lists[0, g * GROUP + k]] for k in range(GROUP)]
        s = [swap_halves(x) for x in v]
        even = [jnp.where(low, v[0], s[1]), jnp.where(low, v[2], s[3])]
        odd = [jnp.where(low, s[0], v[1]), jnp.where(low, s[2], v[3])]
        return jnp.concatenate([jnp.concatenate(even, axis=1), jnp.concatenate(odd, axis=1)], axis=0)

    def rhs_fwd(h, g):
        return jnp.concatenate([src[h][lists[1, g * GROUP + k]] for k in range(GROUP)], axis=0)

    def lhs_bwd(g):
        w = jnp.concatenate([m[lists[4, g * GROUP + k]] for k in range(GROUP)], axis=0).T
        return jnp.concatenate([w[:BLOCK], w[BLOCK:]], axis=1)

    def rhs_bwd(h, g):
        v = [gh[h][lists[5, g * GROUP + k]] for k in range(GROUP)]
        return jnp.concatenate([x[:BLOCK // 2] for x in v] + [x[BLOCK // 2:] for x in v], axis=0)

    def products(h, lhs, rhs, flags, groups, pieces):
        state = [jnp.zeros((BLOCK, LANES), f32)]
        turns = groups // UNROLL

        def body(i, run):
            prods = []
            for u in range(UNROLL):
                g = i * UNROLL + u
                prods.append((g, jnp.dot(lhs(g), rhs(h, g), preferred_element_type=f32)))
            for g, p in prods:
                run = jnp.where(lists[flags, g] > 0, p, run + p)
                runs[g] = run.astype(bf16)
            return run

        def piece(i):
            lo, hi = turns * i // pieces, turns * (i + 1) // pieces
            state[0] = lax.fori_loop(lo, hi, body, state[0])

        return [step_of(piece, i) for i in range(pieces)]

    def settle(dst, h, lasts, groups, blocks):
        runs[groups] = jnp.zeros((BLOCK, LANES), bf16)

        def body(i, _):
            for u in range(8):
                dst[h, i * 8 + u] = runs[lists[lasts, i * 8 + u]]
            return 0

        lax.fori_loop(0, blocks // 8, body, 0)

    nk = 4
    ck = nbd // nk
    chunks = range(nk)
    kind_a, kind_b = chunks[:1], chunks[1:]
    ca = len(kind_a) * ck
    way_of = lambda k: "R" if k % 2 == 0 else "L"
    cut = lambda k: pl.ds(k * ck, ck)
    blk_cut = lambda b, k: pl.ds(b * nbd + k * ck, ck)

    class Sums:
        def __init__(self, tag, to, base, ref, bufs):
            self.tag, self.to, self.base, self.ref = tag, to, base, ref
            (self.ya_out, self.ya_in, self.o_out, self.o_in, self.n_out, self.t_out,
             self.r_in, self.l_in, self.s_out, self.y_in) = bufs
            self.inn = {"R": self.r_in, "L": self.l_in}
            self.got = set()

        def ya(self, h, d):
            if self.ref is not None:
                spot = self.ref(h, 1, d, None)
            else:
                for k in kind_a:
                    self.ya_out[h, d % RING, cut(k)] = self.base(h, 1, d, k).astype(bf16)
                spot = self.ya_out.at[h, d % RING, pl.ds(0, ca)]
            wire.push((self.tag, h, "ya", d % RING), spot, self.ya_in.at[h, d % RING, pl.ds(0, ca)], self.to["Y"])

        def term(self, h, p, d, k):
            if k in kind_b:
                return self.base(h, p, d, k)
            key = (self.tag, h, "ya", d % RING)
            if key not in self.got:
                self.got.add(key)
                wire.take(key, self.ya_in.at[h, d % RING, pl.ds(0, ca)], any_dev)
            return self.base(h, 0, d, k) + f(self.ya_in[h, d % RING, cut(k)])

        def ps(self, k):
            return (0,) if k in kind_a else (1, 0)

        def _out(self, h, p, d, k, buf):
            if self.ref is not None and k in kind_b:
                return self.ref(h, p, d, k)
            buf[h, p, cut(k)] = self.term(h, p, d, k).astype(bf16)
            return buf.at[h, p, cut(k)]

        def far(self, h, k):
            for p in self.ps(k):
                wire.push((self.tag, h, "opp", p, k), self._out(h, p, 2, k, self.o_out), self.o_in.at[h, p, cut(k)],
                          self.to[way_of(k)])

        def near(self, h, k):
            w = other[way_of(k)]
            for p in self.ps(k):
                wire.push((self.tag, h, w, p, k), self._out(h, p, side[w], k, self.n_out), self.inn[w].at[h, p, cut(k)],
                          self.to[w])

        def ring(self, h, k):
            w = way_of(k)
            for p in self.ps(k):
                own = self.term(h, p, side[w], k)
                wire.take((self.tag, h, "opp", p, k), self.o_in.at[h, p, cut(k)], any_dev)
                self.t_out[h, p, cut(k)] = (own + f(self.o_in[h, p, cut(k)])).astype(bf16)
                wire.push((self.tag, h, w, p, k), self.t_out.at[h, p, cut(k)], self.inn[w].at[h, p, cut(k)], self.to[w])

        def total(self, h, p, k):
            own = self.term(h, p, 0, k)
            for w in "RL":
                wire.take((self.tag, h, w, p, k), self.inn[w].at[h, p, cut(k)], any_dev)
            return own + f(self.r_in[h, p, cut(k)]) + f(self.l_in[h, p, cut(k)])

        def pair(self, h, k):
            if k in kind_b:
                self.s_out[h, cut(k)] = self.total(h, 1, k).astype(bf16)
                wire.push((self.tag, h, "y", k), self.s_out.at[h, cut(k)], self.y_in.at[h, cut(k)], self.to["Y"])

        def end(self, h, k):
            value = self.total(h, 0, k)
            if k in kind_b:
                wire.take((self.tag, h, "y", k), self.y_in.at[h, cut(k)], any_dev)
                value = value + f(self.y_in[h, cut(k)])
            return value.astype(bf16)

        def begin(self, h):
            return ([step_of(self.ya, h, 2)] + [step_of(self.far, h, k) for k in kind_b]
                    + [step_of(self.ya, h, d) for d in (1, -1)] + [step_of(self.near, h, k) for k in kind_b]
                    + [step_of(self.ya, h, 0)])

        def second(self, h):
            return [step_of(self.far, h, k) for k in kind_a] + [step_of(self.near, h, k) for k in kind_a]

    def c_base(h, p, d, k):
        return f(part[h, blk_cut(cblk(p, d), k)])

    def c_ref(h, p, d, k):
        return part.at[h, pl.ds(cblk(p, d) * nbd, ca) if k is None else blk_cut(cblk(p, d), k)]

    cs = Sums("c", col_to, c_base, c_ref, c_bufs)

    def c_end(h, k):
        hid[h, cut(k)] = cs.end(h, k)

    rows = ck * BLOCK
    i0 = lax.broadcasted_iota(i32, (rows, rows), 0)
    i1 = lax.broadcasted_iota(i32, (rows, rows), 1)
    inside = i0 % BLOCK
    node = i0 - inside + jnp.where(inside < BLOCK // 2, 2 * inside, 2 * inside - (BLOCK - 1))
    order = (node == i1).astype(f32).astype(bf16)

    def g_push(h, k):
        for way in "YRL":
            wire.push(("g", h, way, 0, 0, k), gl.at[h, cut(k)], gh[h].at[blk_cut(cblk(0, 0), k)], col_to[way])

    def g_pass(h, p, d, k, way, hop):
        spot = gh[h].at[blk_cut(cblk(p, d), k)]
        wire.push(("g", h, way, p, hop, k), spot, spot, col_to[way])

    def dense(k):
        hidden = jnp.concatenate([hid[h, cut(k)].reshape(rows, LANES) for h in (0, 1)], axis=1)
        w = weight[...]
        at = pl.ds(k * rows, rows)
        pre = jnp.dot(hidden, w, preferred_element_type=f32)
        go = jnp.dot(order, gout[at], preferred_element_type=f32)
        act, slope = gelu_both(pre)
        gp = (go * slope).astype(bf16)
        local = lax.dot_general(gp, w, (((1,), (1,)), ((), ())), preferred_element_type=f32).astype(bf16)
        for h in (0, 1):
            mine = local[:, h * LANES:(h + 1) * LANES].reshape(ck, BLOCK, LANES)
            gl[h, cut(k)] = mine
        g_push(0, k)
        for h in (0, 1):
            gh[h][blk_cut(cblk(0, 0), k)] = gl[h, cut(k)]
        out[at] = lax.dot_general(order, act.astype(bf16), (((0,), (0,)), ((), ())),
                                  preferred_element_type=f32).astype(bf16)
        t = lax.dot_general(hidden, gp, (((0,), (0,)), ((), ())), preferred_element_type=f32)
        if k == 0:
            term[...] = t
        else:
            term[...] += t

    def g_pair(h, k):
        wire.take(("g", h, "Y", 0, 0, k), gh[h].at[blk_cut(cblk(1, 0), k)], any_dev)
        if k in kind_b:
            for way in "RL":
                g_pass(h, 1, 0, k, way, 0)

    def g_ring(h, k):
        for p in (0,) if k in kind_a else (0, 1):
            for way in "RL":
                d = -side[way]
                wire.take(("g", h, way, p, 0, k), gh[h].at[blk_cut(cblk(p, d), k)], any_dev)
                if way == way_of(k):
                    g_pass(h, p, d, k, way, 1)
                if k in kind_a:
                    g_pass(h, p, d, k, "Y", d)

    def g_far(h, k):
        for p in (0,) if k in kind_a else (0, 1):
            wire.take(("g", h, way_of(k), p, 1, k), gh[h].at[blk_cut(cblk(p, 2), k)], any_dev)
            if k in kind_a:
                g_pass(h, p, 2, k, "Y", 2)

    def g_last(h):
        for k in kind_a:
            for d in (1, -1, 2):
                wire.take(("g", h, "Y", 0, d, k), gh[h].at[blk_cut(cblk(1, d), k)], any_dev)

    rel = lambda p, d: p * RING + d % RING
    arrived = set()

    def sib_push(h):
        for d in (2, 1, -1, 0):
            for p in (1, 0):
                there = pl.ds(rblk(p, d, 1) * nbd, nbd)
                wire.push(("s", h, rel(p, d)), back.at[h, there], sib_in.at[h, rel(p, d)], row_to["S"])

    def r_base(h, p, d, k):
        key = ("s", h, rel(p, d))
        if key not in arrived:
            arrived.add(key)
            wire.take(key, sib_in.at[h, rel(p, d)], any_dev)
        return f(back[h, blk_cut(rblk(p, d), k)]) + f(sib_in[h, rel(p, d), cut(k)])

    rs = Sums("r", row_to, r_base, None, r_bufs)

    def r_end(h, k):
        gfeat[pl.ds(k * rows, rows), h * LANES:(h + 1) * LANES] = rs.end(h, k).reshape(rows, LANES)

    half = term.shape[0] // 2
    eighth = half // (2 * RING)
    hd = lambda c: pl.ds(pl.multiple_of(c * half, half), half)
    seat = lambda p, d: rblk(p, d) // 2
    sd = lambda j: pl.ds(pl.multiple_of(j * eighth, eighth), eighth)
    spot_of = lambda p, d: pl.ds(pl.multiple_of(core * half + seat(p, d) * eighth, eighth), eighth)

    def w0():
        wire.push("w0", term.at[hd(1 - core)], w_sib, row_to["S"])

    def w1():
        wire.take("w0", w_sib, any_dev)
        w_half[...] = term[hd(core)] + w_sib[...]
        for i, (p, d) in enumerate(peers):
            wire.push(("w1", i), w_half.at[sd(seat(p, d))], w_row.at[i], rdev(p, d))

    def w2():
        mine = w_half[sd(seat(0, 0))]
        for i, _ in enumerate(peers):
            wire.take(("w1", i), w_row.at[i], any_dev)
            mine = mine + w_row[i]
        w_sum[...] = mine
        here = cblk(0, 0)
        w_col[here] = mine
        for i, (p, d) in enumerate(peers):
            wire.push(("w2", i), w_sum, w_col.at[here], cdev(p, d))

    def w3():
        for i, (p, d) in enumerate(peers):
            wire.take(("w2", i), w_col.at[cblk(p, -d)], any_dev)
        total = w_col[0]
        for i in range(1, 2 * RING):
            total = total + w_col[i]
        w_full[spot_of(0, 0)] = total
        for i, (p, d) in enumerate(peers):
            wire.push(("w3", i), w_full.at[spot_of(0, 0)], w_full.at[spot_of(0, 0)], rdev(p, d))

    def w4():
        for i, (p, d) in enumerate(peers):
            wire.take(("w3", i), w_full.at[spot_of(p, -d)], any_dev)
        wire.push("w4", w_full.at[hd(core)], w_full.at[hd(core)], row_to["S"])

    def w5():
        wire.take("w4", w_full.at[hd(1 - core)], any_dev)
        gw[...] = w_full[...]

    loads[0].wait()
    for h in (0, 1):
        src[h][pl.ds(rblk(0, 0) * nbd, nbd)] = feat[:, h * LANES:(h + 1) * LANES].reshape(nbd, BLOCK, LANES)
    met()
    own0, steps0 = gather(0)
    own1, steps1 = gather(1)
    own0()
    loads[1].wait()
    for s in range(0, tiles, 16):
        m[s:s + 16] = vals[s:s + 16].reshape((16,) + m.shape[1:])
    m[tiles:] = jnp.zeros((1,) + m.shape[1:], bf16)
    for i, step in enumerate(steps0):
        step()
        if i == 8:
            own1()

    def each(fn, h, ks):
        for k in ks:
            fn(h, k)

    def run(steps):
        for step in steps:
            step()

    work = products(0, lhs_fwd, rhs_fwd, 2, gf, 3)
    work[0]()
    run(steps1[:5])
    work[1]()
    run(steps1[5:9])
    work[2]()
    settle(part, 0, 3, gf, nr)
    run(cs.begin(0))
    run(steps1[9:])
    work = products(1, lhs_fwd, rhs_fwd, 2, gf, 3)
    work[0]()
    each(cs.ring, 0, kind_b)
    run(cs.second(0))
    work[1]()
    work[2]()
    settle(part, 1, 3, gf, nr)
    run(cs.begin(1))
    each(cs.ring, 0, kind_a)
    each(cs.pair, 0, kind_b)
    for load in loads[2:]:
        load.wait()
    each(cs.ring, 1, kind_b)
    run(cs.second(1))
    each(c_end, 0, chunks)
    each(cs.ring, 1, kind_a)
    each(cs.pair, 1, kind_b)
    for k in chunks:
        c_end(1, k)
        dense(k)
    w0()
    each(g_pair, 0, kind_b)
    each(g_ring, 0, chunks[:2])
    each(g_far, 0, kind_a)
    each(g_ring, 0, chunks[2:])
    each(g_push, 1, chunks)
    each(g_pair, 0, kind_a)
    each(g_far, 0, kind_b)
    g_last(0)
    work = products(0, lhs_bwd, rhs_bwd, 6, gb, 3)
    work[0]()
    w1()
    each(g_pair, 1, kind_b)
    each(g_ring, 1, kind_a)
    work[1]()
    each(g_far, 1, kind_a)
    each(g_ring, 1, kind_b)
    w2()
    work[2]()
    settle(back, 0, 7, gb, nc)
    sib_push(0)
    each(g_pair, 1, kind_a)
    each(g_far, 1, kind_b)
    g_last(1)
    run(rs.begin(0))
    work = products(1, lhs_bwd, rhs_bwd, 6, gb, 3)
    work[0]()
    run(rs.second(0))
    w3()
    work[1]()
    each(rs.ring, 0, kind_b)
    work[2]()
    settle(back, 1, 7, gb, nc)
    sib_push(1)
    each(rs.ring, 0, kind_a)
    each(rs.pair, 0, kind_b)
    run(rs.begin(1))
    w4()
    each(rs.ring, 1, kind_b)
    run(rs.second(1))
    each(r_end, 0, chunks)
    each(rs.ring, 1, kind_a)
    each(rs.pair, 1, kind_b)
    each(r_end, 1, chunks)
    w5()
    wire.drain()


def place_kernel(*refs):
    count = len(refs) // 2
    for i in range(count):
        refs[count + i][...] = refs[i][...]


def place(*arrays):
    n = len(arrays)
    return pl.pallas_call(
        place_kernel,
        out_shape=[jax.ShapeDtypeStruct(a.shape, a.dtype) for a in arrays],
        in_specs=[pl.BlockSpec(memory_space=VM)] * n,
        out_specs=[pl.BlockSpec(memory_space=VM)] * n,
        compiler_params=pltpu.CompilerParams(vmem_limit_bytes=60 << 20),
        name="place",
    )(*arrays)


def layer(lists, features, weight, grad_out, values, nr, nc):
    rows, width = features.shape
    tiles = values.shape[0]
    nbd = rows // BLOCK
    gmax = max(group_bound(tiles, nr), group_bound(tiles, nc))
    wrows = weight.shape[0]
    piece = lambda *lead: pltpu.VMEM(lead + (BLOCK, LANES), bf16)
    wf = lambda *lead: pltpu.VMEM(lead + (wrows,), f32)
    eighth = wrows // (4 * RING)
    two = 2
    two_ring = piece(two, 2, nbd)
    sums = [piece(two, RING, nbd // 2)] * 2 + [two_ring] * 6 + [piece(two, nbd)] * 2
    scratch = [
        pltpu.VMEM(features.shape, bf16), pltpu.VMEM(weight.shape, bf16), pltpu.VMEM(grad_out.shape, bf16),
        pltpu.VMEM(values.shape, bf16), pltpu.VMEM((tiles + 1, BLOCK // 2, 2 * BLOCK), bf16),
        piece(nc), piece(nc), piece(gmax + 1), piece(two, nr),
        sums, piece(two, nbd), piece(two, nbd), piece(nr), piece(nr), piece(two, nc),
        piece(two, 2 * RING, nbd), sums,
        wf(wrows), wf(wrows // 2), wf(wrows // 2), wf(2 * RING - 1, eighth), wf(2 * RING, eighth), wf(eighth), wf(wrows),
        pltpu.SemaphoreType.DMA((400,)), pltpu.SemaphoreType.DMA((400,)), pltpu.SemaphoreType.DMA((4,)),
    ]
    return pl.pallas_call(
        layer_kernel,
        out_shape=[jax.ShapeDtypeStruct((rows, width), bf16), jax.ShapeDtypeStruct((rows, width), bf16),
                   jax.ShapeDtypeStruct((wrows, width), f32)],
        in_specs=[pl.BlockSpec(memory_space=pltpu.SMEM)] + [pl.BlockSpec(memory_space=pl.ANY)] * 4,
        out_specs=[pl.BlockSpec(memory_space=VM)] * 3,
        scratch_shapes=scratch,
        compiler_params=pltpu.CompilerParams(collective_id=1, has_side_effects=True, vmem_limit_bytes=58 << 20),
        name="layer",
    )(lists, features, weight, grad_out, values)


def per_device(features, weight, grad_out, tile_rows, tile_cols, tile_values, tile_counts):
    nodes_dev = features.shape[0]
    nr = nodes_dev * lax.axis_size("col") // BLOCK
    nc = nodes_dev * lax.axis_size("row") // BLOCK
    values = tile_values.reshape(tile_values.shape[2:])
    lists = make_lists(tile_rows, tile_cols, tile_counts, nr, nc)
    return tuple(place(*layer(lists, features, weight, grad_out, values, nr, nc)))


def solution(mesh):
    placed = (
        P(("col", "row"), None),
        P(),
        P(("row", "col"), None),
        P("row", "col", None),
        P("row", "col", None),
        P("row", "col", None, None),
        P("row", "col"),
    )
    return jax.shard_map(
        per_device,
        mesh=mesh,
        in_specs=placed,
        out_specs=(P(("row", "col"), None), P(("col", "row"), None), P()),
        check_vma=False,
    )
```

```python
import functools

import jax
import jax.numpy as jnp
from jax import lax
from jax.experimental import pallas as pl
from jax.experimental.pallas import tpu as pltpu
from jax.sharding import PartitionSpec as P

BLOCK = 64
GROUP = 4
UNROLL = 16
RING = 4
LANES = 128
MESH = pl.DeviceIdType.MESH
VM = pltpu.VMEM
f32, bf16, i32 = jnp.float32, jnp.bfloat16, jnp.int32


def up(n, m):
    return -(-n // m) * m


def group_bound(tiles, blocks):
    return up((tiles + (GROUP - 1) * min(blocks, tiles)) // GROUP, UNROLL)


def lists_of(key_row, other_row, tiles, nb, groups_max, wide):
    tp = key_row.shape[1]
    nbp = up(nb, LANES)
    hot = (lax.broadcasted_iota(i32, (nbp, tp), 0) == key_row).astype(f32)
    hotb = hot.astype(bf16)
    count = jnp.sum(hot, axis=1, keepdims=True)
    upper = (lax.broadcasted_iota(i32, (tp, tp), 0) < lax.broadcasted_iota(i32, (tp, tp), 1)).astype(f32).astype(bf16)
    rank = jnp.dot(hotb, upper, preferred_element_type=f32)
    groups = jnp.floor((count + (GROUP - 1)) * (1.0 / GROUP))
    b0 = lax.broadcasted_iota(i32, (nbp, nbp), 0)
    b1 = lax.broadcasted_iota(i32, (nbp, nbp), 1)
    lower = (b1 < b0).astype(f32).astype(bf16)
    first = jnp.dot(lower, jnp.broadcast_to(groups, (nbp, LANES)).astype(bf16), preferred_element_type=f32)[:, :1]
    place = jnp.sum(hot * (rank + GROUP * first), axis=0, keepdims=True)
    live = jnp.sum(hot, axis=0, keepdims=True) > 0
    place = jnp.where(live, place, -1.0).astype(i32)
    spot = (lax.broadcasted_iota(i32, (wide, tp), 0) == place).astype(f32).astype(bf16)
    t = lax.broadcasted_iota(i32, (1, tp), 1)
    row = lax.broadcasted_iota(i32, (8, tp), 0)
    data = jnp.where(row == 0, t // 128, jnp.where(row == 1, t % 128, jnp.where(row == 2, other_row, 1)))
    got = lax.dot_general(data.astype(f32).astype(bf16), spot, (((1,), (1,)), ((), ())), preferred_element_type=f32)
    there = got[3:4] > 0
    tile = jnp.where(there, got[0:1] * 128 + got[1:2], float(tiles)).astype(i32)
    other = jnp.where(there, got[2:3], 0.0).astype(i32)
    g = lax.broadcasted_iota(i32, (nbp, wide), 1).astype(f32)
    starts = jnp.sum(jnp.where(jnp.logical_and(first == g, groups > 0), 1.0, 0.0), axis=0, keepdims=True).astype(i32)
    last = jnp.where(groups > 0, first + groups - 1, float(groups_max))
    last = jnp.sum(jnp.where(b0 == b1, last, 0.0), axis=0, keepdims=True).astype(i32)
    last = jnp.concatenate([last, jnp.zeros((1, wide - nbp), i32)], axis=1)
    return [tile, other, starts, last]


def lists_kernel(tiles, nr, nc, rows_in, cols_in, count_ref, out_ref, t_rows, t_cols, keep, sems):
    loads = [pltpu.make_async_copy(rows_in, t_rows, sems.at[0]), pltpu.make_async_copy(cols_in, t_cols, sems.at[1])]
    for load in loads:
        load.start()
    keep[...] = jnp.zeros_like(keep)
    for load in loads:
        load.wait()
    wide = out_ref.shape[1]
    keep[0:1, :tiles] = t_rows[0]
    keep[1:2, :tiles] = t_cols[0]
    rows, cols = keep[0:1], keep[1:2]
    live = lax.broadcasted_iota(i32, rows.shape, 1) < count_ref[0, 0]
    fwd = lists_of(jnp.where(live, rows, 4096), cols, tiles, nr, group_bound(tiles, nr), wide)
    bwd = lists_of(jnp.where(live, cols, 4096), rows, tiles, nc, group_bound(tiles, nc), wide)
    for i, v in enumerate(fwd + bwd):
        out_ref[i:i + 1] = v


def make_lists(rows, cols, count, nr, nc):
    tiles = rows.shape[-1]
    wide = up(GROUP * max(group_bound(tiles, nr), group_bound(tiles, nc)), LANES)
    return pl.pallas_call(
        functools.partial(lists_kernel, tiles, nr, nc),
        out_shape=jax.ShapeDtypeStruct((8, wide), i32),
        in_specs=[pl.BlockSpec(memory_space=pl.ANY)] * 2 + [pl.BlockSpec(memory_space=pltpu.SMEM)],
        out_specs=pl.BlockSpec(memory_space=VM),
        scratch_shapes=[pltpu.VMEM(rows.shape, i32), pltpu.VMEM(cols.shape, i32), pltpu.VMEM((8, up(tiles, LANES)), i32),
                        pltpu.SemaphoreType.DMA((2,))],
        compiler_params=pltpu.CompilerParams(vmem_limit_bytes=60 << 20),
        name="lists",
    )(rows, cols, count)


class Wire:
    def __init__(self, send_sem, recv_sem):
        self.send_sem, self.recv_sem = send_sem, recv_sem
        self.ids, self.sent = {}, []

    def _sems(self, key):
        n = self.ids.setdefault(key, len(self.ids))
        assert n < self.send_sem.shape[0]
        return dict(send_sem=self.send_sem.at[n], recv_sem=self.recv_sem.at[n])

    def push(self, key, src, dst, dev):
        copy = pltpu.make_async_remote_copy(
            src_ref=src, dst_ref=dst, device_id=dev, device_id_type=MESH, **self._sems(key))
        copy.start()
        self.sent.append(copy)

    def take(self, key, dst, dev):
        pltpu.make_async_remote_copy(
            src_ref=dst, dst_ref=dst, device_id=dev, device_id_type=MESH, **self._sems(key)).wait_recv()

    def drain(self):
        for copy in self.sent:
            copy.wait_send()


def greet(devs):
    sem = pltpu.get_barrier_semaphore()
    for dev in devs:
        pl.semaphore_signal(sem, inc=1, device_id=dev, device_id_type=MESH)
    return lambda: pl.semaphore_wait(sem, len(devs))


def row_place():
    r = lax.axis_index("row")
    pair, ring, core = r // (2 * RING), (r // 2) % RING, r % 2

    def blk(p, d, s=0):
        return (pair + p) % 2 * (2 * RING) + (ring + d) % RING * 2 + (core + s) % 2

    return blk, (lambda p, d, s=0: {"row": blk(p, d, s)}), core


def col_place():
    c = lax.axis_index("col")
    pair, ring = c // RING, c % RING

    def blk(p, d):
        return (pair + p) % 2 * RING + (ring + d) % RING

    return blk, (lambda p, d: {"col": blk(p, d)})


def gelu_both(z):
    c, a = 0.7978845608, 0.044715
    z2 = z * z
    t = jnp.tanh(c * (z + a * z * z2))
    half = 0.5 * (1.0 + t)
    slope = half + 0.5 * z * (1.0 - t * t) * (c * (1.0 + 3.0 * a * z2))
    return z * half, slope


def swap_halves(m):
    return jnp.concatenate([m[:, BLOCK:], m[:, :BLOCK]], axis=1)


def step_of(fn, *args):
    return lambda: fn(*args)


def layer_kernel(lists, feat_in, weight_in, gout_in, values_in, out, gfeat, gw,
                 feat, weight, gout, vals, m, src_0, src_1, runs, part,
                 c_bufs, hid, gl, gh_0, gh_1, back, sib_in, r_bufs,
                 term, w_sib, w_half, w_row, w_col, w_sum, w_full,
                 send_sem, recv_sem, load_sem):
    rblk, rdev, core = row_place()
    cblk, cdev = col_place()
    wire = Wire(send_sem, recv_sem)
    peers = [(p, d) for p in (0, 1) for d in range(RING) if (p, d) != (0, 0)]
    met = greet([rdev(0, 0, 1)] + [rdev(p, d) for p, d in peers] + [cdev(p, d) for p, d in peers])
    loads = [pltpu.make_async_copy(a, b, load_sem.at[i]) for i, (a, b) in enumerate([
        (feat_in, feat), (values_in, vals), (weight_in, weight), (gout_in, gout)])]
    for load in loads:
        load.start()

    f = lambda v: v.astype(f32)
    src, gh = (src_0, src_1), (gh_0, gh_1)
    tiles = vals.shape[0]
    nbd = feat.shape[0] // BLOCK
    nr, nc = part.shape[1], src_0.shape[0]
    gf, gb = group_bound(tiles, nr), group_bound(tiles, nc)
    row_to = {"R": rdev(0, 1), "L": rdev(0, -1), "Y": rdev(1, 0), "S": rdev(0, 0, 1)}
    col_to = {"R": cdev(0, 1), "L": cdev(0, -1), "Y": cdev(1, 0)}
    any_dev = row_to["S"]
    side = {"R": 1, "L": -1}
    other = {"R": "L", "L": "R"}

    nk = 6
    ck = nbd // nk
    chunks = range(nk)
    kind_a, kind_b = chunks[:2], chunks[2:]
    way_of = lambda k: "R" if k % 2 == 0 else "L"
    cut = lambda k: pl.ds(k * ck, ck)
    blk_cut = lambda b, k: pl.ds(b * nbd + k * ck, ck)

    def gather(h):
        def slot(p, d, s, k):
            return src[h].at[blk_cut(rblk(p, d, s), k)]

        def push(way, p, d, k):
            spot = slot(p, d, 0, k)
            wire.push(("f", h, way, p, d % RING, k), spot, spot, row_to[way])

        def take(way, p, d, k):
            key = ("f", h, way, p, d % RING, k)
            if way == "S":
                wire.take(key, slot(p, d, 1, k), any_dev)
                return
            q, e = {"R": (p, d - 1), "L": (p, d + 1), "Y": (1 - p, d)}[way]
            wire.take(key, slot(q, e, 0, k), any_dev)
            if way == "Y":
                if k in kind_b:
                    push("R", q, e, k)
                    push("L", q, e, k)
            else:
                if abs(e) == 1 and way == way_of(k):
                    push(way, q, e, k)
                if k in kind_a:
                    push("Y", q, e, k)
            push("S", q, e, k)

        def own():
            for k in kind_b:
                push("Y", 0, 0, k)
            for k in chunks:
                push("R", 0, 0, k)
                push("L", 0, 0, k)
            for k in chunks:
                push("S", 0, 0, k)

        def own_late():
            for k in kind_a:
                push("Y", 0, 0, k)

        def far(p, k):
            take(*(("R", p, -1, k) if way_of(k) == "R" else ("L", p, 1, k)))

        def close():
            for key in [key for key in wire.ids if key[:3] == ("f", h, "S")]:
                take("S", *key[3:])

        near = lambda p, k: [step_of(take, way, p, 0, k) for way in "RL"]
        early = [step_of(take, "Y", 0, 0, k) for k in kind_b]
        for i, k in enumerate(kind_a):
            early[3 * i + 1:3 * i + 1] = near(0, k)
        early.append(own_late)
        middle = [x for k in kind_b for x in near(0, k)] + [step_of(far, 0, k) for k in kind_a]
        late = [x for k in kind_b for x in near(1, k)]
        rest = [step_of(take, "Y", 0, 0, k) for k in kind_a]
        rest += [step_of(take, "Y", 0, d, k) for k in kind_a for d in (-1, 1)]
        rest += [step_of(far, 0, k) for k in kind_b] + [step_of(far, 1, k) for k in kind_b]
        rest += [step_of(take, "Y", 0, 2, k) for k in kind_a] + [close]
        return own, early, middle, late, rest

    low = lax.broadcasted_iota(i32, (BLOCK // 2, 2 * BLOCK), 1) < BLOCK

    def lhs_fwd(g):
        v = [m[lists[0, g * GROUP + k]] for k in range(GROUP)]
        s = [swap_halves(x) for x in v]
        even = [jnp.where(low, v[0], s[1]), jnp.where(low, v[2], s[3])]
        odd = [jnp.where(low, s[0], v[1]), jnp.where(low, s[2], v[3])]
        return jnp.concatenate([jnp.concatenate(even, axis=1), jnp.concatenate(odd, axis=1)], axis=0)

    def rhs_fwd(h, g):
        return jnp.concatenate([src[h][lists[1, g * GROUP + k]] for k in range(GROUP)], axis=0)

    def lhs_bwd(g):
        w = jnp.concatenate([m[lists[4, g * GROUP + k]] for k in range(GROUP)], axis=0).T
        return jnp.concatenate([w[:BLOCK], w[BLOCK:]], axis=1)

    def rhs_bwd(h, g):
        v = [gh[h][lists[5, g * GROUP + k]] for k in range(GROUP)]
        return jnp.concatenate([x[:BLOCK // 2] for x in v] + [x[BLOCK // 2:] for x in v], axis=0)

    def products(h, lhs, rhs, flags, groups, pieces):
        state = [jnp.zeros((BLOCK, LANES), f32)]
        turns = groups // UNROLL

        def body(i, run):
            prods = []
            for u in range(UNROLL):
                g = i * UNROLL + u
                prods.append((g, jnp.dot(lhs(g), rhs(h, g), preferred_element_type=f32)))
            for g, p in prods:
                run = jnp.where(lists[flags, g] > 0, p, run + p)
                runs[g] = run.astype(bf16)
            return run

        def piece(i):
            lo, hi = turns * i // pieces, turns * (i + 1) // pieces
            state[0] = lax.fori_loop(lo, hi, body, state[0])

        return [step_of(piece, i) for i in range(pieces)]

    def settle(dst, h, lasts, groups, blocks):
        runs[groups] = jnp.zeros((BLOCK, LANES), bf16)

        def body(i, _):
            for u in range(8):
                dst[h, i * 8 + u] = runs[lists[lasts, i * 8 + u]]
            return 0

        lax.fori_loop(0, blocks // 8, body, 0)

    class Sums:
        def __init__(self, tag, to, base, ref, bufs):
            self.tag, self.to, self.base, self.ref = tag, to, base, ref
            (self.ya_out, self.ya_in, self.o_out, self.o_in, self.n_out, self.t_out,
             self.r_in, self.l_in, self.s_out, self.y_in) = bufs
            self.inn = {"R": self.r_in, "L": self.l_in}
            self.got = set()

        def kinds(self, h):
            n = 2 - h
            return chunks[:n], chunks[n:]

        def ya(self, h, d):
            size = len(self.kinds(h)[0]) * ck
            if self.ref is not None:
                spot = self.ref(h, 1, d, 0, size)
            else:
                for k in self.kinds(h)[0]:
                    self.ya_out[h, d % RING, cut(k)] = self.base(h, 1, d, k).astype(bf16)
                spot = self.ya_out.at[h, d % RING, pl.ds(0, size)]
            wire.push((self.tag, h, "ya", d % RING), spot, self.ya_in.at[h, d % RING, pl.ds(0, size)], self.to["Y"])

        def term(self, h, p, d, k):
            kind_a, kind_b = self.kinds(h)
            if k in kind_b:
                return self.base(h, p, d, k)
            key = (self.tag, h, "ya", d % RING)
            if key not in self.got:
                self.got.add(key)
                wire.take(key, self.ya_in.at[h, d % RING, pl.ds(0, len(kind_a) * ck)], any_dev)
            return self.base(h, 0, d, k) + f(self.ya_in[h, d % RING, cut(k)])

        def ps(self, h, k):
            return (0,) if k in self.kinds(h)[0] else (1, 0)

        def _out(self, h, p, d, k, buf):
            if self.ref is not None and k in self.kinds(h)[1]:
                return self.ref(h, p, d, k)
            buf[h, p, cut(k)] = self.term(h, p, d, k).astype(bf16)
            return buf.at[h, p, cut(k)]

        def far(self, h, k):
            for p in self.ps(h, k):
                wire.push((self.tag, h, "opp", p, k), self._out(h, p, 2, k, self.o_out), self.o_in.at[h, p, cut(k)],
                          self.to[way_of(k)])

        def near(self, h, k):
            w = other[way_of(k)]
            for p in self.ps(h, k):
                wire.push((self.tag, h, w, p, k), self._out(h, p, side[w], k, self.n_out), self.inn[w].at[h, p, cut(k)],
                          self.to[w])

        def ring(self, h, k):
            w = way_of(k)
            for p in self.ps(h, k):
                own = self.term(h, p, side[w], k)
                wire.take((self.tag, h, "opp", p, k), self.o_in.at[h, p, cut(k)], any_dev)
                self.t_out[h, p, cut(k)] = (own + f(self.o_in[h, p, cut(k)])).astype(bf16)
                wire.push((self.tag, h, w, p, k), self.t_out.at[h, p, cut(k)], self.inn[w].at[h, p, cut(k)], self.to[w])

        def total(self, h, p, k):
            own = self.term(h, p, 0, k)
            for w in "RL":
                wire.take((self.tag, h, w, p, k), self.inn[w].at[h, p, cut(k)], any_dev)
            return own + f(self.r_in[h, p, cut(k)]) + f(self.l_in[h, p, cut(k)])

        def pair(self, h, k):
            if k in self.kinds(h)[1]:
                self.s_out[h, cut(k)] = self.total(h, 1, k).astype(bf16)
                wire.push((self.tag, h, "y", k), self.s_out.at[h, cut(k)], self.y_in.at[h, cut(k)], self.to["Y"])

        def end(self, h, k):
            value = self.total(h, 0, k)
            if k in self.kinds(h)[1]:
                wire.take((self.tag, h, "y", k), self.y_in.at[h, cut(k)], any_dev)
                value = value + f(self.y_in[h, cut(k)])
            return value.astype(bf16)

        def begin(self, h):
            kind_b = self.kinds(h)[1]
            steps = [step_of(self.ya, h, d) for d in (2, 1, -1)] + [step_of(self.far, h, k) for k in kind_b]
            steps += [step_of(self.ya, h, 0)]
            return steps, [step_of(self.near, h, k) for k in kind_b]

        def second(self, h):
            kind_a = self.kinds(h)[0]
            return [step_of(self.far, h, k) for k in kind_a] + [step_of(self.near, h, k) for k in kind_a]

    def c_base(h, p, d, k):
        return f(part[h, blk_cut(cblk(p, d), k)])

    def c_ref(h, p, d, k, size=ck):
        return part.at[h, pl.ds(cblk(p, d) * nbd + k * ck, size)]

    cs = Sums("c", col_to, c_base, c_ref, c_bufs)

    def c_end(h, k):
        hid[h, cut(k)] = cs.end(h, k)

    rows = ck * BLOCK
    i0 = lax.broadcasted_iota(i32, (rows, rows), 0)
    i1 = lax.broadcasted_iota(i32, (rows, rows), 1)
    inside = i0 % BLOCK
    node = i0 - inside + jnp.where(inside < BLOCK // 2, 2 * inside, 2 * inside - (BLOCK - 1))
    order = (node == i1).astype(f32).astype(bf16)

    def g_push(h, ks, ways):
        for k in ks:
            for way in ways:
                wire.push(("g", h, way, 0, 0, k), gl.at[h, cut(k)], gh[h].at[blk_cut(cblk(0, 0), k)], col_to[way])

    def g_pass(h, p, d, k, way, hop):
        spot = gh[h].at[blk_cut(cblk(p, d), k)]
        wire.push(("g", h, way, p, hop, k), spot, spot, col_to[way])

    def dense(k):
        hidden = jnp.concatenate([hid[h, cut(k)].reshape(rows, LANES) for h in (0, 1)], axis=1)
        w = weight[...]
        at = pl.ds(k * rows, rows)
        pre = jnp.dot(hidden, w, preferred_element_type=f32)
        go = jnp.dot(order, gout[at], preferred_element_type=f32)
        act, slope = gelu_both(pre)
        gp = (go * slope).astype(bf16)
        local = lax.dot_general(gp, w, (((1,), (1,)), ((), ())), preferred_element_type=f32).astype(bf16)
        for h in (0, 1):
            mine = local[:, h * LANES:(h + 1) * LANES].reshape(ck, BLOCK, LANES)
            gl[h, cut(k)] = mine
        g_push(0, (k,), "YRL")
        for h in (0, 1):
            gh[h][blk_cut(cblk(0, 0), k)] = gl[h, cut(k)]
        out[at] = lax.dot_general(order, act.astype(bf16), (((0,), (0,)), ((), ())),
                                  preferred_element_type=f32).astype(bf16)
        t = lax.dot_general(hidden, gp, (((0,), (0,)), ((), ())), preferred_element_type=f32)
        if k == 0:
            term[...] = t
        else:
            term[...] += t

    def g_pair(h, k):
        wire.take(("g", h, "Y", 0, 0, k), gh[h].at[blk_cut(cblk(1, 0), k)], any_dev)
        if k in kind_b:
            for way in "RL":
                g_pass(h, 1, 0, k, way, 0)

    def g_ring(h, k):
        for p in (0,) if k in kind_a else (0, 1):
            for way in "RL":
                d = -side[way]
                wire.take(("g", h, way, p, 0, k), gh[h].at[blk_cut(cblk(p, d), k)], any_dev)
                if way == way_of(k):
                    g_pass(h, p, d, k, way, 1)
                if k in kind_a:
                    g_pass(h, p, d, k, "Y", d)

    def g_far(h, k):
        for p in (0,) if k in kind_a else (0, 1):
            wire.take(("g", h, way_of(k), p, 1, k), gh[h].at[blk_cut(cblk(p, 2), k)], any_dev)
            if k in kind_a:
                g_pass(h, p, 2, k, "Y", 2)

    def g_last(h):
        for k in kind_a:
            for d in (1, -1, 2):
                wire.take(("g", h, "Y", 0, d, k), gh[h].at[blk_cut(cblk(1, d), k)], any_dev)

    rel = lambda p, d: p * RING + d % RING
    arrived = set()

    def sib_push(h):
        for d in (2, 1, -1, 0):
            for p in (1, 0):
                there = pl.ds(rblk(p, d, 1) * nbd, nbd)
                wire.push(("s", h, rel(p, d)), back.at[h, there], sib_in.at[h, rel(p, d)], row_to["S"])

    def r_base(h, p, d, k):
        key = ("s", h, rel(p, d))
        if key not in arrived:
            arrived.add(key)
            wire.take(key, sib_in.at[h, rel(p, d)], any_dev)
        return f(back[h, blk_cut(rblk(p, d), k)]) + f(sib_in[h, rel(p, d), cut(k)])

    rs = Sums("r", row_to, r_base, None, r_bufs)

    def r_end(h, k):
        gfeat[pl.ds(k * rows, rows), h * LANES:(h + 1) * LANES] = rs.end(h, k).reshape(rows, LANES)

    half = term.shape[0] // 2
    eighth = half // (2 * RING)
    hd = lambda c: pl.ds(pl.multiple_of(c * half, half), half)
    seat = lambda p, d: rblk(p, d) // 2
    sd = lambda j: pl.ds(pl.multiple_of(j * eighth, eighth), eighth)
    spot_of = lambda p, d: pl.ds(pl.multiple_of(core * half + seat(p, d) * eighth, eighth), eighth)

    def w0():
        wire.push("w0", term.at[hd(1 - core)], w_sib, row_to["S"])

    def w1():
        wire.take("w0", w_sib, any_dev)
        w_half[...] = term[hd(core)] + w_sib[...]
        for i, (p, d) in enumerate(peers):
            wire.push(("w1", i), w_half.at[sd(seat(p, d))], w_row.at[i], rdev(p, d))

    def w2():
        mine = w_half[sd(seat(0, 0))]
        for i, _ in enumerate(peers):
            wire.take(("w1", i), w_row.at[i], any_dev)
            mine = mine + w_row[i]
        w_sum[...] = mine
        here = cblk(0, 0)
        w_col[here] = mine
        for i, (p, d) in enumerate(peers):
            wire.push(("w2", i), w_sum, w_col.at[here], cdev(p, d))

    def w3():
        for i, (p, d) in enumerate(peers):
            wire.take(("w2", i), w_col.at[cblk(p, -d)], any_dev)
        total = w_col[0]
        for i in range(1, 2 * RING):
            total = total + w_col[i]
        w_full[spot_of(0, 0)] = total
        for i, (p, d) in enumerate(peers):
            wire.push(("w3", i), w_full.at[spot_of(0, 0)], w_full.at[spot_of(0, 0)], rdev(p, d))

    def w4():
        for i, (p, d) in enumerate(peers):
            wire.take(("w3", i), w_full.at[spot_of(p, -d)], any_dev)
        wire.push("w4", w_full.at[hd(core)], w_full.at[hd(core)], row_to["S"])

    def w5():
        wire.take("w4", w_full.at[hd(1 - core)], any_dev)
        gw[...] = w_full[...]

    loads[0].wait()
    for h in (0, 1):
        src[h][pl.ds(rblk(0, 0) * nbd, nbd)] = feat[:, h * LANES:(h + 1) * LANES].reshape(nbd, BLOCK, LANES)
    met()
    own0, *steps0 = gather(0)
    own1, *steps1 = gather(1)
    own0()
    loads[1].wait()
    for s in range(0, tiles, 16):
        m[s:s + 16] = vals[s:s + 16].reshape((16,) + m.shape[1:])
    m[tiles:] = jnp.zeros((1,) + m.shape[1:], bf16)
    def each(fn, h, ks):
        for k in ks:
            fn(h, k)

    def run(steps):
        for step in steps:
            step()

    run(steps0[0] + steps0[1] + steps0[2])
    own1()
    run(steps0[3])
    early, middle, late, rest = steps1
    some_a, some_b = cs.kinds(1)
    work = products(0, lhs_fwd, rhs_fwd, 2, gf, 7)
    turns = [early, middle[:4], middle[4:8], late[:4], late[4:], middle[8:], []]
    for piece, steps in zip(work, turns):
        piece()
        run(steps)
    settle(part, 0, 3, gf, nr)
    run(sum(cs.begin(0), []))
    run(rest)
    work = products(1, lhs_fwd, rhs_fwd, 2, gf, 3)
    work[0]()
    each(cs.ring, 0, cs.kinds(0)[1])
    run(cs.second(0))
    work[1]()
    work[2]()
    each(cs.ring, 0, cs.kinds(0)[0])
    settle(part, 1, 3, gf, nr)
    run(sum(cs.begin(1), []))
    each(cs.pair, 0, cs.kinds(0)[1])
    for load in loads[2:]:
        load.wait()
    each(cs.ring, 1, some_b[:1])
    run(cs.second(1))
    each(cs.ring, 1, some_b[1:3])
    each(c_end, 0, chunks)
    each(cs.ring, 1, some_a)
    each(cs.ring, 1, some_b[3:])
    each(cs.pair, 1, cs.kinds(1)[1])
    for k in chunks:
        c_end(1, k)
        dense(k)
    w0()
    each(g_ring, 0, kind_a)
    each(g_pair, 0, kind_b)
    each(g_ring, 0, kind_b[:2])
    each(g_far, 0, kind_a)
    each(g_ring, 0, kind_b[2:])
    g_push(1, kind_b, "Y")
    g_push(1, chunks, "RL")
    g_push(1, kind_a, "Y")
    each(g_pair, 0, kind_a)
    each(g_far, 0, kind_b)
    g_last(0)
    work = products(0, lhs_bwd, rhs_bwd, 6, gb, 5)
    work[0]()
    each(g_ring, 1, kind_a)
    each(g_pair, 1, kind_b)
    w1()
    work[1]()
    each(g_ring, 1, kind_b[:2])
    work[2]()
    each(g_far, 1, kind_a)
    each(g_ring, 1, kind_b[2:])
    work[3]()
    w2()
    work[4]()
    settle(back, 0, 7, gb, nc)
    sib_push(0)
    each(g_pair, 1, kind_a)
    each(g_far, 1, kind_b)
    g_last(1)
    run(sum(rs.begin(0), []))
    work = products(1, lhs_bwd, rhs_bwd, 6, gb, 3)
    work[0]()
    w3()
    work[1]()
    run(rs.second(0))
    each(rs.ring, 0, rs.kinds(0)[1])
    work[2]()
    each(rs.ring, 0, rs.kinds(0)[0])
    settle(back, 1, 7, gb, nc)
    sib_push(1)
    some, more = rs.begin(1)
    run(some + rs.second(1) + more)
    each(rs.pair, 0, rs.kinds(0)[1])
    w4()
    each(rs.ring, 1, some_b[:3])
    each(rs.ring, 1, some_a)
    each(rs.ring, 1, some_b[3:])
    each(r_end, 0, chunks)
    each(rs.pair, 1, rs.kinds(1)[1])
    each(r_end, 1, chunks)
    w5()
    wire.drain()


def place_kernel(*refs):
    count = len(refs) // 2
    for i in range(count):
        refs[count + i][...] = refs[i][...]


def place(*arrays):
    n = len(arrays)
    return pl.pallas_call(
        place_kernel,
        out_shape=[jax.ShapeDtypeStruct(a.shape, a.dtype) for a in arrays],
        in_specs=[pl.BlockSpec(memory_space=VM)] * n,
        out_specs=[pl.BlockSpec(memory_space=VM)] * n,
        compiler_params=pltpu.CompilerParams(vmem_limit_bytes=60 << 20),
        name="place",
    )(*arrays)


def layer(lists, features, weight, grad_out, values, nr, nc):
    rows, width = features.shape
    tiles = values.shape[0]
    nbd = rows // BLOCK
    gmax = max(group_bound(tiles, nr), group_bound(tiles, nc))
    wrows = weight.shape[0]
    piece = lambda *lead: pltpu.VMEM(lead + (BLOCK, LANES), bf16)
    wf = lambda *lead: pltpu.VMEM(lead + (wrows,), f32)
    eighth = wrows // (4 * RING)
    two = 2
    two_ring = piece(two, 2, nbd)
    sums = [piece(two, RING, nbd // 3)] * 2 + [two_ring] * 6 + [piece(two, nbd)] * 2
    scratch = [
        pltpu.VMEM(features.shape, bf16), pltpu.VMEM(weight.shape, bf16), pltpu.VMEM(grad_out.shape, bf16),
        pltpu.VMEM(values.shape, bf16), pltpu.VMEM((tiles + 1, BLOCK // 2, 2 * BLOCK), bf16),
        piece(nc), piece(nc), piece(gmax + 1), piece(two, nr),
        sums, piece(two, nbd), piece(two, nbd), piece(nr), piece(nr), piece(two, nc),
        piece(two, 2 * RING, nbd), sums,
        wf(wrows), wf(wrows // 2), wf(wrows // 2), wf(2 * RING - 1, eighth), wf(2 * RING, eighth), wf(eighth), wf(wrows),
        pltpu.SemaphoreType.DMA((512,)), pltpu.SemaphoreType.DMA((512,)), pltpu.SemaphoreType.DMA((4,)),
    ]
    return pl.pallas_call(
        layer_kernel,
        out_shape=[jax.ShapeDtypeStruct((rows, width), bf16), jax.ShapeDtypeStruct((rows, width), bf16),
                   jax.ShapeDtypeStruct((wrows, width), f32)],
        in_specs=[pl.BlockSpec(memory_space=pltpu.SMEM)] + [pl.BlockSpec(memory_space=pl.ANY)] * 4,
        out_specs=[pl.BlockSpec(memory_space=VM)] * 3,
        scratch_shapes=scratch,
        compiler_params=pltpu.CompilerParams(collective_id=1, has_side_effects=True, vmem_limit_bytes=58 << 20),
        name="layer",
    )(lists, features, weight, grad_out, values)


def per_device(features, weight, grad_out, tile_rows, tile_cols, tile_values, tile_counts):
    nodes_dev = features.shape[0]
    nr = nodes_dev * lax.axis_size("col") // BLOCK
    nc = nodes_dev * lax.axis_size("row") // BLOCK
    values = tile_values.reshape(tile_values.shape[2:])
    lists = make_lists(tile_rows, tile_cols, tile_counts, nr, nc)
    return tuple(place(*layer(lists, features, weight, grad_out, values, nr, nc)))


def solution(mesh):
    placed = (
        P(("col", "row"), None),
        P(),
        P(("row", "col"), None),
        P("row", "col", None),
        P("row", "col", None),
        P("row", "col", None, None),
        P("row", "col"),
    )
    return jax.shard_map(
        per_device,
        mesh=mesh,
        in_specs=placed,
        out_specs=(P(("row", "col"), None), P(("col", "row"), None), P()),
        check_vma=False,
    )
```

```python
import functools

import jax
import jax.numpy as jnp
from jax import lax
from jax.experimental import pallas as pl
from jax.experimental.pallas import tpu as pltpu
from jax.sharding import PartitionSpec as P

BLOCK = 64
GROUP = 4
UNROLL = 32
RING = 4
LANES = 128
MESH = pl.DeviceIdType.MESH
VM = pltpu.VMEM
f32, bf16, i32 = jnp.float32, jnp.bfloat16, jnp.int32


def up(n, m):
    return -(-n // m) * m


def group_bound(tiles, blocks):
    return up((tiles + (GROUP - 1) * min(blocks, tiles)) // GROUP, UNROLL)


def lists_of(key_row, other_row, tiles, nb, groups_max, wide):
    tp = key_row.shape[1]
    nbp = up(nb, LANES)
    hot = (lax.broadcasted_iota(i32, (nbp, tp), 0) == key_row).astype(f32)
    hotb = hot.astype(bf16)
    count = jnp.sum(hot, axis=1, keepdims=True)
    upper = (lax.broadcasted_iota(i32, (tp, tp), 0) < lax.broadcasted_iota(i32, (tp, tp), 1)).astype(f32).astype(bf16)
    rank = jnp.dot(hotb, upper, preferred_element_type=f32)
    groups = jnp.floor((count + (GROUP - 1)) * (1.0 / GROUP))
    b0 = lax.broadcasted_iota(i32, (nbp, nbp), 0)
    b1 = lax.broadcasted_iota(i32, (nbp, nbp), 1)
    lower = (b1 < b0).astype(f32).astype(bf16)
    first = jnp.dot(lower, jnp.broadcast_to(groups, (nbp, LANES)).astype(bf16), preferred_element_type=f32)[:, :1]
    place = jnp.sum(hot * (rank + GROUP * first), axis=0, keepdims=True)
    live = jnp.sum(hot, axis=0, keepdims=True) > 0
    place = jnp.where(live, place, -1.0).astype(i32)
    spot = (lax.broadcasted_iota(i32, (wide, tp), 0) == place).astype(f32).astype(bf16)
    t = lax.broadcasted_iota(i32, (1, tp), 1)
    row = lax.broadcasted_iota(i32, (8, tp), 0)
    data = jnp.where(row == 0, t // 128, jnp.where(row == 1, t % 128, jnp.where(row == 2, other_row, 1)))
    got = lax.dot_general(data.astype(f32).astype(bf16), spot, (((1,), (1,)), ((), ())), preferred_element_type=f32)
    there = got[3:4] > 0
    tile = jnp.where(there, got[0:1] * 128 + got[1:2], float(tiles)).astype(i32)
    other = jnp.where(there, got[2:3], 0.0).astype(i32)
    g = lax.broadcasted_iota(i32, (nbp, wide), 1).astype(f32)
    starts = jnp.sum(jnp.where(jnp.logical_and(first == g, groups > 0), 1.0, 0.0), axis=0, keepdims=True).astype(i32)
    last = jnp.where(groups > 0, first + groups - 1, float(groups_max))
    last = jnp.sum(jnp.where(b0 == b1, last, 0.0), axis=0, keepdims=True).astype(i32)
    last = jnp.concatenate([last, jnp.zeros((1, wide - nbp), i32)], axis=1)
    return [tile, other, starts, last]


def lists_kernel(tiles, nr, nc, rows_in, cols_in, count_ref, out_ref, t_rows, t_cols, keep, sems):
    loads = [pltpu.make_async_copy(rows_in, t_rows, sems.at[0]), pltpu.make_async_copy(cols_in, t_cols, sems.at[1])]
    for load in loads:
        load.start()
    keep[...] = jnp.zeros_like(keep)
    for load in loads:
        load.wait()
    wide = out_ref.shape[1]
    keep[0:1, :tiles] = t_rows[0]
    keep[1:2, :tiles] = t_cols[0]
    rows, cols = keep[0:1], keep[1:2]
    live = lax.broadcasted_iota(i32, rows.shape, 1) < count_ref[0, 0]
    fwd = lists_of(jnp.where(live, rows, 4096), cols, tiles, nr, group_bound(tiles, nr), wide)
    bwd = lists_of(jnp.where(live, cols, 4096), rows, tiles, nc, group_bound(tiles, nc), wide)
    for i, v in enumerate(fwd + bwd):
        out_ref[i:i + 1] = v


def make_lists(rows, cols, count, nr, nc):
    tiles = rows.shape[-1]
    wide = up(GROUP * max(group_bound(tiles, nr), group_bound(tiles, nc)), LANES)
    return pl.pallas_call(
        functools.partial(lists_kernel, tiles, nr, nc),
        out_shape=jax.ShapeDtypeStruct((8, wide), i32),
        in_specs=[pl.BlockSpec(memory_space=pl.ANY)] * 2 + [pl.BlockSpec(memory_space=pltpu.SMEM)],
        out_specs=pl.BlockSpec(memory_space=VM),
        scratch_shapes=[pltpu.VMEM(rows.shape, i32), pltpu.VMEM(cols.shape, i32), pltpu.VMEM((8, up(tiles, LANES)), i32),
                        pltpu.SemaphoreType.DMA((2,))],
        compiler_params=pltpu.CompilerParams(vmem_limit_bytes=60 << 20),
        name="lists",
    )(rows, cols, count)


class Wire:
    def __init__(self, send_sem, recv_sem):
        self.send_sem, self.recv_sem = send_sem, recv_sem
        self.ids, self.sent = {}, []

    def _sems(self, key):
        n = self.ids.setdefault(key, len(self.ids))
        assert n < self.send_sem.shape[0]
        return dict(send_sem=self.send_sem.at[n], recv_sem=self.recv_sem.at[n])

    def push(self, key, src, dst, dev):
        copy = pltpu.make_async_remote_copy(
            src_ref=src, dst_ref=dst, device_id=dev, device_id_type=MESH, **self._sems(key))
        copy.start()
        self.sent.append(copy)

    def take(self, key, dst, dev):
        pltpu.make_async_remote_copy(
            src_ref=dst, dst_ref=dst, device_id=dev, device_id_type=MESH, **self._sems(key)).wait_recv()

    def drain(self):
        for copy in self.sent:
            copy.wait_send()


def greet(devs):
    sem = pltpu.get_barrier_semaphore()
    for dev in devs:
        pl.semaphore_signal(sem, inc=1, device_id=dev, device_id_type=MESH)
    return lambda: pl.semaphore_wait(sem, len(devs))


def row_place():
    r = lax.axis_index("row")
    pair, ring, core = r // (2 * RING), (r // 2) % RING, r % 2

    def blk(p, d, s=0):
        return (pair + p) % 2 * (2 * RING) + (ring + d) % RING * 2 + (core + s) % 2

    return blk, (lambda p, d, s=0: {"row": blk(p, d, s)}), core


def col_place():
    c = lax.axis_index("col")
    pair, ring = c // RING, c % RING

    def blk(p, d):
        return (pair + p) % 2 * RING + (ring + d) % RING

    return blk, (lambda p, d: {"col": blk(p, d)})


def gelu_both(z):
    c, a = 0.7978845608, 0.044715
    z2 = z * z
    t = jnp.tanh(c * (z + a * z * z2))
    half = 0.5 * (1.0 + t)
    slope = half + 0.5 * z * (1.0 - t * t) * (c * (1.0 + 3.0 * a * z2))
    return z * half, slope


def swap_halves(m):
    return jnp.concatenate([m[:, BLOCK:], m[:, :BLOCK]], axis=1)


def step_of(fn, *args):
    return lambda: fn(*args)


def layer_kernel(lists, feat_in, weight_in, gout_in, values_in, out, gfeat, gw,
                 feat, weight, gout, vals, m, src_0, src_1, runs, part,
                 c_bufs, hid, gl, gh_0, gh_1, back, sib_in, r_bufs,
                 term, w_sib, w_half, w_row, w_col, w_sum, w_full,
                 send_sem, recv_sem, load_sem):
    rblk, rdev, core = row_place()
    cblk, cdev = col_place()
    wire = Wire(send_sem, recv_sem)
    peers = [(p, d) for p in (0, 1) for d in range(RING) if (p, d) != (0, 0)]
    loads = [pltpu.make_async_copy(a, b, load_sem.at[i]) for i, (a, b) in enumerate([
        (feat_in, feat), (values_in, vals), (weight_in, weight), (gout_in, gout)])]
    for load in loads:
        load.start()
    met = greet([rdev(0, 0, 1)] + [rdev(p, d) for p, d in peers] + [cdev(p, d) for p, d in peers])

    f = lambda v: v.astype(f32)
    src, gh = (src_0, src_1), (gh_0, gh_1)
    tiles = vals.shape[0]
    nbd = feat.shape[0] // BLOCK
    nr, nc = part.shape[1], src_0.shape[0]
    gf, gb = group_bound(tiles, nr), group_bound(tiles, nc)
    row_to = {"R": rdev(0, 1), "L": rdev(0, -1), "Y": rdev(1, 0), "S": rdev(0, 0, 1)}
    col_to = {"R": cdev(0, 1), "L": cdev(0, -1), "Y": cdev(1, 0)}
    any_dev = row_to["S"]
    side = {"R": 1, "L": -1}
    other = {"R": "L", "L": "R"}

    nk = 6
    ck = nbd // nk
    chunks = range(nk)
    kind_a, kind_b = chunks[:2], chunks[2:]
    way_of = lambda k: "R" if k % 2 == 0 else "L"
    cut = lambda k: pl.ds(k * ck, ck)
    blk_cut = lambda b, k: pl.ds(b * nbd + k * ck, ck)

    def gather(h):
        def slot(p, d, s, k):
            return src[h].at[blk_cut(rblk(p, d, s), k)]

        def push(way, p, d, k):
            spot = slot(p, d, 0, k)
            wire.push(("f", h, way, p, d % RING, k), spot, spot, row_to[way])

        def take(way, p, d, k):
            key = ("f", h, way, p, d % RING, k)
            if way == "S":
                wire.take(key, slot(p, d, 1, k), any_dev)
                return
            q, e = {"R": (p, d - 1), "L": (p, d + 1), "Y": (1 - p, d)}[way]
            wire.take(key, slot(q, e, 0, k), any_dev)
            if way == "Y":
                if k in kind_b:
                    push("R", q, e, k)
                    push("L", q, e, k)
            else:
                if abs(e) == 1 and way == way_of(k):
                    push(way, q, e, k)
                if k in kind_a:
                    push("Y", q, e, k)
            push("S", q, e, k)

        def own():
            for k in kind_b:
                push("Y", 0, 0, k)
            for k in chunks:
                push("R", 0, 0, k)
                push("L", 0, 0, k)
            for k in chunks:
                push("S", 0, 0, k)

        def own_late():
            for k in kind_a:
                push("Y", 0, 0, k)

        def far(p, k):
            take(*(("R", p, -1, k) if way_of(k) == "R" else ("L", p, 1, k)))

        def close():
            for key in [key for key in wire.ids if key[:3] == ("f", h, "S")]:
                take("S", *key[3:])

        near = lambda p, k: [step_of(take, way, p, 0, k) for way in "RL"]
        early = [step_of(take, "Y", 0, 0, k) for k in kind_b]
        for i, k in enumerate(kind_a):
            early[3 * i + 1:3 * i + 1] = near(0, k)
        early.append(own_late)
        middle = [x for k in kind_b for x in near(0, k)] + [step_of(far, 0, k) for k in kind_a]
        late = [x for k in kind_b for x in near(1, k)]
        rest = [step_of(take, "Y", 0, 0, k) for k in kind_a]
        rest += [step_of(take, "Y", 0, d, k) for k in kind_a for d in (-1, 1)]
        rest += [step_of(far, 0, k) for k in kind_b] + [step_of(far, 1, k) for k in kind_b]
        rest += [step_of(take, "Y", 0, 2, k) for k in kind_a] + [close]
        return own, early, middle, late, rest

    low = lax.broadcasted_iota(i32, (BLOCK // 2, 2 * BLOCK), 1) < BLOCK

    def lhs_fwd(g):
        v = [m[lists[0, g * GROUP + k]] for k in range(GROUP)]
        s = [swap_halves(x) for x in v]
        even = [jnp.where(low, v[0], s[1]), jnp.where(low, v[2], s[3])]
        odd = [jnp.where(low, s[0], v[1]), jnp.where(low, s[2], v[3])]
        return jnp.concatenate([jnp.concatenate(even, axis=1), jnp.concatenate(odd, axis=1)], axis=0)

    def rhs_fwd(h, g):
        return jnp.concatenate([src[h][lists[1, g * GROUP + k]] for k in range(GROUP)], axis=0)

    def lhs_bwd(g):
        w = jnp.concatenate([m[lists[4, g * GROUP + k]] for k in range(GROUP)], axis=0).T
        return jnp.concatenate([w[:BLOCK], w[BLOCK:]], axis=1)

    def rhs_bwd(h, g):
        v = [gh[h][lists[5, g * GROUP + k]] for k in range(GROUP)]
        return jnp.concatenate([x[:BLOCK // 2] for x in v] + [x[BLOCK // 2:] for x in v], axis=0)

    def products(h, lhs, rhs, flags, groups, pieces, unroll=UNROLL):
        state = [jnp.zeros((BLOCK, LANES), f32)]
        turns = groups // unroll

        def body(i, run):
            prods = []
            for u in range(unroll):
                g = i * unroll + u
                prods.append((g, jnp.dot(lhs(g), rhs(h, g), preferred_element_type=f32)))
            for g, p in prods:
                run = jnp.where(lists[flags, g] > 0, p, run + p)
                runs[g] = run.astype(bf16)
            return run

        def piece(i):
            lo, hi = turns * i // pieces, turns * (i + 1) // pieces
            state[0] = lax.fori_loop(lo, hi, body, state[0])

        return [step_of(piece, i) for i in range(pieces)]

    def settle(dst, h, lasts, groups, blocks):
        runs[groups] = jnp.zeros((BLOCK, LANES), bf16)

        def body(i, _):
            for u in range(8):
                dst[h, i * 8 + u] = runs[lists[lasts, i * 8 + u]]
            return 0

        lax.fori_loop(0, blocks // 8, body, 0)

    class Sums:
        def __init__(self, tag, to, base, ref, bufs):
            self.tag, self.to, self.base, self.ref = tag, to, base, ref
            (self.ya_out, self.ya_in, self.o_out, self.o_in, self.n_out, self.t_out,
             self.r_in, self.l_in, self.s_out, self.y_in) = bufs
            self.inn = {"R": self.r_in, "L": self.l_in}
            self.got = set()

        def kinds(self, h):
            n = 2 - h
            return chunks[:n], chunks[n:]

        def ya(self, h, d):
            size = len(self.kinds(h)[0]) * ck
            if self.ref is not None:
                spot = self.ref(h, 1, d, 0, size)
            else:
                for k in self.kinds(h)[0]:
                    self.ya_out[h, d % RING, cut(k)] = self.base(h, 1, d, k).astype(bf16)
                spot = self.ya_out.at[h, d % RING, pl.ds(0, size)]
            wire.push((self.tag, h, "ya", d % RING), spot, self.ya_in.at[h, d % RING, pl.ds(0, size)], self.to["Y"])

        def term(self, h, p, d, k):
            kind_a, kind_b = self.kinds(h)
            if k in kind_b:
                return self.base(h, p, d, k)
            key = (self.tag, h, "ya", d % RING)
            if key not in self.got:
                self.got.add(key)
                wire.take(key, self.ya_in.at[h, d % RING, pl.ds(0, len(kind_a) * ck)], any_dev)
            return self.base(h, 0, d, k) + f(self.ya_in[h, d % RING, cut(k)])

        def ps(self, h, k):
            return (0,) if k in self.kinds(h)[0] else (1, 0)

        def _out(self, h, p, d, k, buf):
            if self.ref is not None and k in self.kinds(h)[1]:
                return self.ref(h, p, d, k)
            buf[h, p, cut(k)] = self.term(h, p, d, k).astype(bf16)
            return buf.at[h, p, cut(k)]

        def far(self, h, k):
            for p in self.ps(h, k):
                wire.push((self.tag, h, "opp", p, k), self._out(h, p, 2, k, self.o_out), self.o_in.at[h, p, cut(k)],
                          self.to[way_of(k)])

        def near(self, h, k):
            w = other[way_of(k)]
            for p in self.ps(h, k):
                wire.push((self.tag, h, w, p, k), self._out(h, p, side[w], k, self.n_out), self.inn[w].at[h, p, cut(k)],
                          self.to[w])

        def ring(self, h, k):
            w = way_of(k)
            for p in self.ps(h, k):
                own = self.term(h, p, side[w], k)
                wire.take((self.tag, h, "opp", p, k), self.o_in.at[h, p, cut(k)], any_dev)
                self.t_out[h, p, cut(k)] = (own + f(self.o_in[h, p, cut(k)])).astype(bf16)
                wire.push((self.tag, h, w, p, k), self.t_out.at[h, p, cut(k)], self.inn[w].at[h, p, cut(k)], self.to[w])

        def total(self, h, p, k):
            own = self.term(h, p, 0, k)
            for w in "RL":
                wire.take((self.tag, h, w, p, k), self.inn[w].at[h, p, cut(k)], any_dev)
            return own + f(self.r_in[h, p, cut(k)]) + f(self.l_in[h, p, cut(k)])

        def pair(self, h, k):
            if k in self.kinds(h)[1]:
                self.s_out[h, cut(k)] = self.total(h, 1, k).astype(bf16)
                wire.push((self.tag, h, "y", k), self.s_out.at[h, cut(k)], self.y_in.at[h, cut(k)], self.to["Y"])

        def end(self, h, k):
            value = self.total(h, 0, k)
            if k in self.kinds(h)[1]:
                wire.take((self.tag, h, "y", k), self.y_in.at[h, cut(k)], any_dev)
                value = value + f(self.y_in[h, cut(k)])
            return value.astype(bf16)

        def begin(self, h):
            kind_b = self.kinds(h)[1]
            steps = [step_of(self.ya, h, d) for d in (2, 1, -1)] + [step_of(self.far, h, k) for k in kind_b]
            steps += [step_of(self.ya, h, 0)]
            return steps, [step_of(self.near, h, k) for k in kind_b]

        def second(self, h):
            kind_a = self.kinds(h)[0]
            return [step_of(self.far, h, k) for k in kind_a] + [step_of(self.near, h, k) for k in kind_a]

    def c_base(h, p, d, k):
        return f(part[h, blk_cut(cblk(p, d), k)])

    def c_ref(h, p, d, k, size=ck):
        return part.at[h, pl.ds(cblk(p, d) * nbd + k * ck, size)]

    cs = Sums("c", col_to, c_base, c_ref, c_bufs)

    def c_end(h, k):
        hid[h, cut(k)] = cs.end(h, k)

    rows = ck * BLOCK
    i0 = lax.broadcasted_iota(i32, (rows, rows), 0)
    i1 = lax.broadcasted_iota(i32, (rows, rows), 1)
    inside = i0 % BLOCK
    node = i0 - inside + jnp.where(inside < BLOCK // 2, 2 * inside, 2 * inside - (BLOCK - 1))
    order = (node == i1).astype(f32).astype(bf16)

    def g_push(h, ks, ways):
        for k in ks:
            for way in ways:
                wire.push(("g", h, way, 0, 0, k), gl.at[h, cut(k)], gh[h].at[blk_cut(cblk(0, 0), k)], col_to[way])

    def g_pass(h, p, d, k, way, hop):
        spot = gh[h].at[blk_cut(cblk(p, d), k)]
        wire.push(("g", h, way, p, hop, k), spot, spot, col_to[way])

    def dense(k):
        hidden = jnp.concatenate([hid[h, cut(k)].reshape(rows, LANES) for h in (0, 1)], axis=1)
        w = weight[...]
        at = pl.ds(k * rows, rows)
        pre = jnp.dot(hidden, w, preferred_element_type=f32)
        go = jnp.dot(order, gout[at], preferred_element_type=f32)
        act, slope = gelu_both(pre)
        gp = (go * slope).astype(bf16)
        local = lax.dot_general(gp, w, (((1,), (1,)), ((), ())), preferred_element_type=f32).astype(bf16)
        for h in (0, 1):
            mine = local[:, h * LANES:(h + 1) * LANES].reshape(ck, BLOCK, LANES)
            gl[h, cut(k)] = mine
        g_push(0, (k,), "YRL")
        for h in (0, 1):
            gh[h][blk_cut(cblk(0, 0), k)] = gl[h, cut(k)]
        out[at] = lax.dot_general(order, act.astype(bf16), (((0,), (0,)), ((), ())),
                                  preferred_element_type=f32).astype(bf16)
        t = lax.dot_general(hidden, gp, (((0,), (0,)), ((), ())), preferred_element_type=f32)
        if k == 0:
            term[...] = t
        else:
            term[...] += t

    def g_pair(h, k):
        wire.take(("g", h, "Y", 0, 0, k), gh[h].at[blk_cut(cblk(1, 0), k)], any_dev)
        if k in kind_b:
            for way in "RL":
                g_pass(h, 1, 0, k, way, 0)

    def g_ring(h, k):
        for p in (0,) if k in kind_a else (0, 1):
            for way in "RL":
                d = -side[way]
                wire.take(("g", h, way, p, 0, k), gh[h].at[blk_cut(cblk(p, d), k)], any_dev)
                if way == way_of(k):
                    g_pass(h, p, d, k, way, 1)
                if k in kind_a:
                    g_pass(h, p, d, k, "Y", d)

    def g_far(h, k):
        for p in (0,) if k in kind_a else (0, 1):
            wire.take(("g", h, way_of(k), p, 1, k), gh[h].at[blk_cut(cblk(p, 2), k)], any_dev)
            if k in kind_a:
                g_pass(h, p, 2, k, "Y", 2)

    def g_last(h):
        for k in kind_a:
            for d in (1, -1, 2):
                wire.take(("g", h, "Y", 0, d, k), gh[h].at[blk_cut(cblk(1, d), k)], any_dev)

    rel = lambda p, d: p * RING + d % RING
    arrived = set()

    def sib_push(h):
        for d in (2, 1, -1, 0):
            for p in (1, 0):
                there = pl.ds(rblk(p, d, 1) * nbd, nbd)
                wire.push(("s", h, rel(p, d)), back.at[h, there], sib_in.at[h, rel(p, d)], row_to["S"])

    def r_base(h, p, d, k):
        key = ("s", h, rel(p, d))
        if key not in arrived:
            arrived.add(key)
            wire.take(key, sib_in.at[h, rel(p, d)], any_dev)
        return f(back[h, blk_cut(rblk(p, d), k)]) + f(sib_in[h, rel(p, d), cut(k)])

    rs = Sums("r", row_to, r_base, None, r_bufs)

    def r_end(h, k):
        gfeat[pl.ds(k * rows, rows), h * LANES:(h + 1) * LANES] = rs.end(h, k).reshape(rows, LANES)

    half = term.shape[0] // 2
    eighth = half // (2 * RING)
    hd = lambda c: pl.ds(pl.multiple_of(c * half, half), half)
    seat = lambda p, d: rblk(p, d) // 2
    sd = lambda j: pl.ds(pl.multiple_of(j * eighth, eighth), eighth)
    spot_of = lambda p, d: pl.ds(pl.multiple_of(core * half + seat(p, d) * eighth, eighth), eighth)

    def w0():
        wire.push("w0", term.at[hd(1 - core)], w_sib, row_to["S"])

    def w1():
        wire.take("w0", w_sib, any_dev)
        w_half[...] = term[hd(core)] + w_sib[...]
        for i, (p, d) in enumerate(peers):
            wire.push(("w1", i), w_half.at[sd(seat(p, d))], w_row.at[i], rdev(p, d))

    def w2():
        mine = w_half[sd(seat(0, 0))]
        for i, _ in enumerate(peers):
            wire.take(("w1", i), w_row.at[i], any_dev)
            mine = mine + w_row[i]
        w_sum[...] = mine
        here = cblk(0, 0)
        w_col[here] = mine
        for i, (p, d) in enumerate(peers):
            wire.push(("w2", i), w_sum, w_col.at[here], cdev(p, d))

    def w3():
        for i, (p, d) in enumerate(peers):
            wire.take(("w2", i), w_col.at[cblk(p, -d)], any_dev)
        total = w_col[0]
        for i in range(1, 2 * RING):
            total = total + w_col[i]
        w_full[spot_of(0, 0)] = total
        for i, (p, d) in enumerate(peers):
            wire.push(("w3", i), w_full.at[spot_of(0, 0)], w_full.at[spot_of(0, 0)], rdev(p, d))

    def w4():
        for i, (p, d) in enumerate(peers):
            wire.take(("w3", i), w_full.at[spot_of(p, -d)], any_dev)
        wire.push("w4", w_full.at[hd(core)], w_full.at[hd(core)], row_to["S"])

    def w5():
        wire.take("w4", w_full.at[hd(1 - core)], any_dev)
        gw[...] = w_full[...]

    loads[0].wait()
    for h in (0, 1):
        src[h][pl.ds(rblk(0, 0) * nbd, nbd)] = feat[:, h * LANES:(h + 1) * LANES].reshape(nbd, BLOCK, LANES)
    met()
    own0, *steps0 = gather(0)
    own1, *steps1 = gather(1)
    own0()
    loads[1].wait()
    for s in range(0, tiles, 16):
        m[s:s + 16] = vals[s:s + 16].reshape((16,) + m.shape[1:])
    m[tiles:] = jnp.zeros((1,) + m.shape[1:], bf16)
    def each(fn, h, ks):
        for k in ks:
            fn(h, k)

    def run(steps):
        for step in steps:
            step()

    run(steps0[0] + steps0[1] + steps0[2])
    own1()
    run(steps0[3])
    early, middle, late, rest = steps1
    some_a, some_b = cs.kinds(1)
    work = products(0, lhs_fwd, rhs_fwd, 2, gf, 7)
    turns = [early, middle[:4], middle[4:8], late[:4], late[4:], middle[8:], []]
    for piece, steps in zip(work, turns):
        piece()
        run(steps)
    settle(part, 0, 3, gf, nr)
    run(sum(cs.begin(0), []))
    run(rest)
    work = products(1, lhs_fwd, rhs_fwd, 2, gf, 3, 56)
    work[0]()
    each(cs.ring, 0, cs.kinds(0)[1])
    run(cs.second(0))
    work[1]()
    work[2]()
    each(cs.ring, 0, cs.kinds(0)[0])
    settle(part, 1, 3, gf, nr)
    run(sum(cs.begin(1), []))
    each(cs.pair, 0, cs.kinds(0)[1])
    for load in loads[2:]:
        load.wait()
    each(cs.ring, 1, some_b[:1])
    run(cs.second(1))
    each(cs.ring, 1, some_b[1:3])
    each(c_end, 0, chunks)
    each(cs.ring, 1, some_a)
    each(cs.ring, 1, some_b[3:])
    each(cs.pair, 1, cs.kinds(1)[1])
    for k in chunks:
        c_end(1, k)
        dense(k)
    w0()
    each(g_ring, 0, kind_a)
    each(g_pair, 0, kind_b)
    each(g_ring, 0, kind_b[:2])
    each(g_far, 0, kind_a)
    each(g_ring, 0, kind_b[2:])
    g_push(1, kind_b, "Y")
    g_push(1, chunks, "RL")
    g_push(1, kind_a, "Y")
    each(g_pair, 0, kind_a)
    each(g_far, 0, kind_b)
    g_last(0)
    work = products(0, lhs_bwd, rhs_bwd, 6, gb, 5, 64)
    work[0]()
    each(g_ring, 1, kind_a)
    each(g_pair, 1, kind_b)
    w1()
    work[1]()
    each(g_ring, 1, kind_b[:2])
    work[2]()
    each(g_far, 1, kind_a)
    each(g_ring, 1, kind_b[2:])
    work[3]()
    w2()
    work[4]()
    settle(back, 0, 7, gb, nc)
    sib_push(0)
    each(g_pair, 1, kind_a)
    each(g_far, 1, kind_b)
    g_last(1)
    work = products(1, lhs_bwd, rhs_bwd, 6, gb, 3, 64)
    run(sum(rs.begin(0), []))
    work[0]()
    w3()
    work[1]()
    run(rs.second(0))
    each(rs.ring, 0, rs.kinds(0)[1])
    work[2]()
    each(rs.ring, 0, rs.kinds(0)[0])
    settle(back, 1, 7, gb, nc)
    sib_push(1)
    some, more = rs.begin(1)
    run(some + rs.second(1) + more)
    each(rs.pair, 0, rs.kinds(0)[1])
    w4()
    each(rs.ring, 1, some_b[:3])
    each(rs.ring, 1, some_a)
    each(rs.ring, 1, some_b[3:])
    each(r_end, 0, chunks)
    each(rs.pair, 1, rs.kinds(1)[1])
    each(r_end, 1, chunks)
    w5()
    wire.drain()


def place_kernel(*refs):
    n = len(refs) // 3
    sems = refs[-1]
    into = [pltpu.make_async_copy(refs[i], refs[2 * n + i], sems.at[i]) for i in range(n)]
    onto = [pltpu.make_async_copy(refs[2 * n + i], refs[n + i], sems.at[n + i]) for i in range(n)]
    for copy in into:
        copy.start()
    for i in range(n):
        into[i].wait()
        onto[i].start()
    for copy in onto:
        copy.wait()


def place(*arrays):
    n = len(arrays)
    return pl.pallas_call(
        place_kernel,
        out_shape=[jax.ShapeDtypeStruct(a.shape, a.dtype) for a in arrays],
        in_specs=[pl.BlockSpec(memory_space=pl.ANY)] * n,
        out_specs=[pl.BlockSpec(memory_space=pl.ANY)] * n,
        scratch_shapes=[pltpu.VMEM(a.shape, a.dtype) for a in arrays] + [pltpu.SemaphoreType.DMA((2 * n,))],
        compiler_params=pltpu.CompilerParams(vmem_limit_bytes=60 << 20),
        name="place",
    )(*arrays)


def layer(lists, features, weight, grad_out, values, nr, nc):
    rows, width = features.shape
    tiles = values.shape[0]
    nbd = rows // BLOCK
    gmax = max(group_bound(tiles, nr), group_bound(tiles, nc))
    wrows = weight.shape[0]
    piece = lambda *lead: pltpu.VMEM(lead + (BLOCK, LANES), bf16)
    wf = lambda *lead: pltpu.VMEM(lead + (wrows,), f32)
    eighth = wrows // (4 * RING)
    two = 2
    two_ring = piece(two, 2, nbd)
    sums = [piece(two, RING, nbd // 3)] * 2 + [two_ring] * 6 + [piece(two, nbd)] * 2
    scratch = [
        pltpu.VMEM(features.shape, bf16), pltpu.VMEM(weight.shape, bf16), pltpu.VMEM(grad_out.shape, bf16),
        pltpu.VMEM(values.shape, bf16), pltpu.VMEM((tiles + 1, BLOCK // 2, 2 * BLOCK), bf16),
        piece(nc), piece(nc), piece(gmax + 1), piece(two, nr),
        sums, piece(two, nbd), piece(two, nbd), piece(nr), piece(nr), piece(two, nc),
        piece(two, 2 * RING, nbd), sums,
        wf(wrows), wf(wrows // 2), wf(wrows // 2), wf(2 * RING - 1, eighth), wf(2 * RING, eighth), wf(eighth), wf(wrows),
        pltpu.SemaphoreType.DMA((512,)), pltpu.SemaphoreType.DMA((512,)), pltpu.SemaphoreType.DMA((4,)),
    ]
    return pl.pallas_call(
        layer_kernel,
        out_shape=[jax.ShapeDtypeStruct((rows, width), bf16), jax.ShapeDtypeStruct((rows, width), bf16),
                   jax.ShapeDtypeStruct((wrows, width), f32)],
        in_specs=[pl.BlockSpec(memory_space=pltpu.SMEM)] + [pl.BlockSpec(memory_space=pl.ANY)] * 4,
        out_specs=[pl.BlockSpec(memory_space=VM)] * 3,
        scratch_shapes=scratch,
        compiler_params=pltpu.CompilerParams(collective_id=1, has_side_effects=True, vmem_limit_bytes=58 << 20),
        name="layer",
    )(lists, features, weight, grad_out, values)


def per_device(features, weight, grad_out, tile_rows, tile_cols, tile_values, tile_counts):
    nodes_dev = features.shape[0]
    nr = nodes_dev * lax.axis_size("col") // BLOCK
    nc = nodes_dev * lax.axis_size("row") // BLOCK
    values = tile_values.reshape(tile_values.shape[2:])
    lists = make_lists(tile_rows, tile_cols, tile_counts, nr, nc)
    return tuple(place(*layer(lists, features, weight, grad_out, values, nr, nc)))


def solution(mesh):
    placed = (
        P(("col", "row"), None),
        P(),
        P(("row", "col"), None),
        P("row", "col", None),
        P("row", "col", None),
        P("row", "col", None, None),
        P("row", "col"),
    )
    return jax.shard_map(
        per_device,
        mesh=mesh,
        in_specs=placed,
        out_specs=(P(("row", "col"), None), P(("col", "row"), None), P()),
        check_vma=False,
    )
```
